32 devices in a mesh: groups: 2 (over y), tensor: 4 (over z), expert: 2 (over x), sub: 2 (over core).
Axes of the slice: x: 2, y: 2, z: 4, core: 2. Of those that a mesh axis runs over, the one named last changes fastest.
Arguments:
- tokens: bfloat16 [1024, 3072], P(('groups', 'expert', 'sub'), 'tensor'), parts along dimension 0, may hold values from -6 to 6
- cotangent: bfloat16 [1024, 3072], P(('groups', 'expert', 'sub'), 'tensor'), parts along dimension 0, may hold values from -6 to 6
- expert_ids: int32 [1024, 2], P(('groups', 'expert', 'sub')), parts along dimension 0, may hold values from 0 to 3, all different within a row; in each aligned block of 128 rows (0 to 127, 128 to 255, ...) at most 80 rows name the same one
- gate_values: float32 [1024, 2], P(('groups', 'expert', 'sub')), parts along dimension 0, may hold values from 0.2 to 1
- w_gate: bfloat16 [4, 3072, 16384], P('expert', 'sub', 'tensor'), may hold values from -0.15625 to 0.15625
- w_up: bfloat16 [4, 3072, 16384], P('expert', 'sub', 'tensor'), may hold values from -0.15625 to 0.15625
- w_down: bfloat16 [4, 16384, 3072], P('expert', 'tensor', 'sub'), may hold values from -0.0625 to 0.0625
Outputs:
- mixed: bfloat16 [1024, 3072], P(('groups', 'expert', 'sub'), 'tensor'), parts along dimension 0
- token_grad: bfloat16 [1024, 3072], P(('groups', 'expert', 'sub'), 'tensor'), parts along dimension 0
The draws below stay inside these ranges and needn't reach their ends.
There are 2 independent parts, one for each index of `groups`. The reference program is written for one: setup_inputs(seed, part) draws one part's arguments, and reference() takes and returns one part's arrays. A program takes and returns all parts, laid end to end along the dimension named above; an argument that names none is the same for every part. Nothing has to cross between parts.
Inputs may be any that keep to these rules, and one draw needn't show every extreme that they name: `expert_ids`: each row names 2 different experts. Within each aligned block of 128 rows no expert is named by more than 80 rows, and in some block one expert is named by exactly 80 rows.
All inputs are finite; a program needn't handle non-finite values.
Results may differ from the reference program's by a relative error of at most 0.012.
Values may be sent and summed in bfloat16 or wider, within the bound.
No kernel may reach another device: no remote copies, remote signals or barrier semaphores. Data moves between devices by JAX's collectives and lax.ppermute only.
A program may use at most 448 MiB of HBM per device.

```python
import math
import jax
import jax.numpy as jnp
import numpy as np
from jax import lax

D = 3072
FF = 16384
EXPERTS = 4
TOP = 2
TOK_DEV = 128
CAP = 80
TOKENS = 512
N_TENSOR = 4


def raised(entries, stream_key, source, target, shards_of, factor):
    def block_of(axis_at):
        return (jnp.arange(entries.shape[axis_at]) // (entries.shape[axis_at] // shards_of)).reshape((-1,) + (1,) * (entries.ndim - 1 - axis_at))

    one_side = jax.random.permutation(stream_key, shards_of)[block_of(target)]
    far = (block_of(target) + shards_of // 2) % shards_of
    return jnp.where((block_of(source) == one_side) | (block_of(source) == far), factor * entries, entries)


def level_of(own_key, dims, split, smallest, high):
    def one(axis_at, shards_of):
        steps = jax.random.uniform(jax.random.fold_in(jax.random.fold_in(own_key, 6), axis_at), (shards_of,), jnp.float32, smallest / len(split), high / len(split))
        return jnp.repeat(jnp.exp(steps), dims[axis_at] // shards_of).reshape((-1,) + (1,) * (len(dims) - axis_at - 1))

    level = one(*split[0])
    for cut in split[1:]:
        level = level * one(*cut)
    return level


def assign_block(stream_key, own, number, rows, count, top, limit, slope):
    ranking = jax.random.permutation(stream_key, count)
    packed, ordinary = shares(count, rows * top, limit, slope, True), shares(count, rows * top, limit, slope, False)
    places = jnp.arange(count)

    def named(lengths, offset_by):
        used = int((lengths > 0).sum())
        fixed = max(1, used // 4)
        moved = fixed + (places - fixed + offset_by * (used - fixed)) % max(1, count - fixed)
        return jnp.zeros((count,), jnp.int32).at[ranking[jnp.where(places < fixed, places, moved)]].set(jnp.asarray(lengths, jnp.int32))

    lengths = jnp.where(number % 4 == 0, named(packed, number // 4), named(ordinary, number - number // 4 - 1))
    mixed = jax.random.permutation(jax.random.fold_in(own, 3), count)
    source_of, sink = mixed[0:count // 2 * 2:2], mixed[1:count // 2 * 2:2]
    room = jnp.minimum(lengths[source_of] - 1, limit - lengths[sink]) // 2
    room = jnp.where((source_of == ranking[0]) | (sink == ranking[0]) | (lengths[sink] == 0), 0, jnp.maximum(room, 0))
    moved = jax.random.randint(jax.random.fold_in(own, 4), (count // 2,), 0, 1 << 20) % (room + 1)
    lengths = lengths.at[source_of].add(-moved).at[sink].add(moved)
    labels = jnp.searchsorted(jnp.cumsum(lengths), jnp.arange(rows * top), side="right").astype(jnp.int32)
    table = labels.reshape(top, rows).T
    table = table[jax.random.permutation(jax.random.fold_in(own, 1), rows)]
    offset_by = jax.random.randint(jax.random.fold_in(own, 2), (rows, 1), 0, top)
    return jnp.take_along_axis(table, (jnp.arange(top)[None, :] + offset_by) % top, axis=1)


def shares(number_of, total, reach, slope, full):
    portions = [(1 << 20) // math.isqrt(grade ** slope) + 1 for grade in range(1, number_of + 1)]
    largest = reach if full else min(reach, max(-(-total // number_of), total * portions[0] // sum(portions)))
    least = 1 if total - largest >= number_of - 1 else 0
    counts, surplus = [largest] + [least] * (number_of - 1), total - largest - least * (number_of - 1)
    while surplus > 0:
        free = [i for i in range(1, number_of) if counts[i] < largest] or [i for i in range(1, number_of) if counts[i] < reach]
        mass, remaining = sum([portions[i] for i in free]), surplus
        for i in free:
            extra = min(reach - counts[i], max(1, remaining * portions[i] // mass), surplus)
            counts[i] = counts[i] + extra
            surplus = surplus - extra
    return np.array(counts)


def scatter_about(rng, dims, scale, most, shards=(), kind=jnp.bfloat16):
    loudness = level_of(rng, dims, shards, -0.22, 0.18) if shards else 1.0
    result = jax.random.normal(rng, dims, jnp.float32) * scale * loudness
    return jnp.minimum(jnp.maximum(result, -most), most).astype(kind)


def bell_draw_with(stream_key, dims, deviation, limit, split, heavy, kind=jnp.bfloat16):
    result = deviation * jax.random.normal(stream_key, dims, jnp.float32)
    if split:
        result = result * level_of(stream_key, dims, split, -0.22, 0.18)
    return jnp.clip(raised(result, jax.random.fold_in(stream_key, 3), *heavy), -limit, limit).astype(kind)


def setup_inputs(seed: int = 0, part: int = 0) -> dict:
    key_of = jax.random.split(jax.random.key(seed), 8)
    part_splits = jax.random.split(jax.random.fold_in(key_of[7], part), 8)
    tokens = scatter_about(part_splits[0], (TOKENS, D), 1.0, 6.0, ((0, 4), (1, 4)))
    cotangent = scatter_about(part_splits[1], (TOKENS, D), 1.0, 6.0, ((0, 4), (1, 4)))
    expert_ids_keys = jax.random.split(jax.random.fold_in(part_splits[2], 1), TOKENS // TOK_DEV)
    expert_ids_turns = jax.random.permutation(jax.random.fold_in(part_splits[2], 3), TOKENS // TOK_DEV)
    expert_ids = jax.vmap(lambda own, number: assign_block(jax.random.fold_in(part_splits[2], 2), own, number, TOK_DEV, EXPERTS, TOP, CAP, 2))(expert_ids_keys, expert_ids_turns).reshape((TOKENS, TOP))
    gate_values = jnp.clip(0.2 + 0.8 * jax.random.uniform(part_splits[3], (TOKENS, TOP), jnp.float32) ** level_of(part_splits[3], (TOKENS, TOP), ((0, 4),), -0.2, 0.2), 0.2, 1.0)
    w_gate = bell_draw_with(key_of[4], (EXPERTS, D, FF), D ** -0.5, 0.15625, ((0, 2), (1, 2), (2, 4)), (2, 1, 4, 2.0))
    w_up = bell_draw_with(key_of[5], (EXPERTS, D, FF), D ** -0.5, 0.15625, ((0, 2), (1, 2), (2, 4)), (2, 1, 4, 2.0))
    w_down = bell_draw_with(key_of[6], (EXPERTS, FF, D), FF ** -0.5, 0.0625, ((0, 2), (1, 4), (2, 2)), (1, 2, 4, 2.0))
    return dict(tokens=tokens, cotangent=cotangent, expert_ids=expert_ids, gate_values=gate_values, w_gate=w_gate, w_up=w_up, w_down=w_down)


def expert_pass(tokens, cotangent, gate_matrix, up_matrix, down_matrix):
    block_width = FF // N_TENSOR
    gate_pre = jnp.dot(tokens, gate_matrix, preferred_element_type=jnp.float32)
    up_pre = jnp.dot(tokens, up_matrix, preferred_element_type=jnp.float32)
    hidden_grad = jnp.dot(cotangent, down_matrix.T, preferred_element_type=jnp.float32)
    sigmoid = jax.nn.sigmoid(gate_pre)
    hidden = (gate_pre * sigmoid * up_pre).astype(jnp.bfloat16)
    up_grad = (hidden_grad * gate_pre * sigmoid).astype(jnp.bfloat16)
    gate_grad = (hidden_grad * up_pre * sigmoid * (1.0 + gate_pre * (1.0 - sigmoid))).astype(jnp.bfloat16)

    def add_block(totals, block_index):
        offset = block_index * block_width
        hidden_block = lax.dynamic_slice_in_dim(hidden, offset, block_width, 1)
        gate_block = lax.dynamic_slice_in_dim(gate_grad, offset, block_width, 1)
        up_block = lax.dynamic_slice_in_dim(up_grad, offset, block_width, 1)
        down_rows = lax.dynamic_slice_in_dim(down_matrix, offset, block_width, 0)
        gate_cols = lax.dynamic_slice_in_dim(gate_matrix, offset, block_width, 1)
        up_cols = lax.dynamic_slice_in_dim(up_matrix, offset, block_width, 1)
        out_part = jnp.dot(hidden_block, down_rows, preferred_element_type=jnp.float32)
        back_part = jnp.dot(gate_block, gate_cols.T, preferred_element_type=jnp.float32) + jnp.dot(
            up_block, up_cols.T, preferred_element_type=jnp.float32)
        out_part = out_part.astype(jnp.bfloat16).astype(jnp.float32)
        back_part = back_part.astype(jnp.bfloat16).astype(jnp.float32)
        return (totals[0] + out_part, totals[1] + back_part), None

    zero_rows = jnp.zeros((tokens.shape[0], D), jnp.float32)
    sums, ignored = lax.scan(add_block, (zero_rows, zero_rows), jnp.arange(N_TENSOR, dtype=jnp.int32))
    return sums[0].astype(jnp.bfloat16), sums[1].astype(jnp.bfloat16)


def reference(tokens, cotangent, expert_ids, gate_values, w_gate, w_up, w_down):
    mixed = jnp.zeros((TOKENS, D), jnp.float32)
    token_grad = jnp.zeros((TOKENS, D), jnp.float32)
    for expert in range(EXPERTS):
        weight = jnp.sum(jnp.where(expert_ids == expert, gate_values, jnp.zeros_like(gate_values)), axis=1)[:, None]
        out_rows, back_rows = expert_pass(tokens, cotangent, w_gate[expert], w_up[expert], w_down[expert])
        mixed = mixed + weight * out_rows.astype(jnp.float32)
        token_grad = token_grad + weight * back_rows.astype(jnp.float32)
    return mixed.astype(jnp.bfloat16), token_grad.astype(jnp.bfloat16)
```

```python
import functools

import jax
import jax.numpy as jnp
from jax import lax
from jax.experimental import pallas as pl
from jax.experimental.pallas import tpu as pltpu
from jax.sharding import PartitionSpec as P

EXPERTS = 4
CAP = 80
BF16 = jnp.bfloat16
F32 = jnp.float32
VMEM_BYTES = 48 * 1024 * 1024


def slot_ranks(expert_ids, experts):
    flat_ids = expert_ids.reshape(-1)
    onehot = (flat_ids[:, None] == jnp.arange(experts, dtype=jnp.int32)[None, :]).astype(jnp.int32)
    earlier = jnp.cumsum(onehot, axis=0) - onehot
    return jnp.sum(earlier * onehot, axis=1).reshape(expert_ids.shape)


def swap(value, axis):
    return lax.ppermute(value, axis, [(0, 1), (1, 0)])


def across(value, distance):
    return lax.ppermute(value, "tensor", [(i, i ^ distance) for i in range(lax.axis_size("tensor"))])


def nt(a, b):
    return lax.dot_general(a, b, (((1,), (1,)), ((), ())), preferred_element_type=F32)


class Place:
    def __init__(self):
        self.sources = lax.axis_size("expert")
        self.tensors = lax.axis_size("tensor")
        self.small = self.sources == 2 and self.tensors == 4
        self.expert = lax.axis_index("expert")
        self.sub = lax.axis_index("sub")
        self.tensor = lax.axis_index("tensor")
        self.blocks = 2 * self.sources
        self.index = jnp.stack([self.expert, self.sub, self.tensor]).astype(jnp.int32)


def pieces_of(small, blocks, index_ref, width):
    if not small:
        return [(block, 0) for block in range(blocks)]
    expert, sub, tensor = index_ref[0], index_ref[1], index_ref[2]
    found = []
    for sub_far in range(2):
        for expert_far in range(2):
            for low_far in range(2):
                at_expert = expert + expert_far - 2 * expert * expert_far
                at_sub = sub + sub_far - 2 * sub * sub_far
                low = lax.rem(tensor, 2)
                low = low + low_far - 2 * low * low_far
                found.append((at_expert * 2 + at_sub, low * width))
    return found


def gather_rows(place, rows):
    if place.small:
        near = [rows] + [across(rows, k) for k in (1, 2, 3)]
        far = [swap(block, "expert") for block in near]
        high = (place.tensor // 2 + place.sub) % 2 == 1
        low_half = jnp.stack([near[0], near[1], far[0], far[1]])
        high_half = jnp.stack([near[2], near[3], far[2], far[3]])
        keep = jnp.where(high, high_half, low_half)
        send = jnp.where(high, low_half, high_half)
        return [keep, swap(send, "sub")]
    count = rows.shape[0]
    whole = lax.all_gather(rows, ("tensor", "expert"))
    whole = whole.reshape(place.tensors, place.sources, count, rows.shape[1])
    whole = whole.transpose(1, 2, 0, 3).reshape(place.sources, count, 2, -1)
    halves = (whole[:, :, 0], whole[:, :, 1])
    first = place.sub == 0
    keep = jnp.where(first, halves[0], halves[1])
    got = swap(jnp.where(first, halves[1], halves[0]), "sub")
    both = jnp.where(first, jnp.stack([keep, got], 1), jnp.stack([got, keep], 1))
    return [both.reshape((2 * place.sources, count, -1))]


def scatter_rows(place, parts):
    if place.small:
        kept, same_far, core_near, core_far = parts
        from_far = swap(same_far, "expert")
        from_core = swap(core_near, "sub")
        from_both = lax.ppermute(core_far, ("expert", "sub"), [(i, 3 - i) for i in range(4)])
        own_half = kept.astype(F32) + from_far.astype(F32)
        other_half = from_core.astype(F32) + from_both.astype(F32)
        high = (place.tensor // 2 + place.sub) % 2 == 1
        near_pair = jnp.where(high, other_half, own_half).astype(BF16)
        far_pair = jnp.where(high, own_half, other_half).astype(BF16)
        width = near_pair.shape[1] // 2
        total = near_pair[:, :width].astype(F32)
        total = total + across(near_pair[:, width:], 1).astype(F32)
        total = total + across(far_pair[:, :width], 2).astype(F32)
        total = total + across(far_pair[:, width:], 3).astype(F32)
        return total.astype(BF16)
    stacked = jnp.stack(parts)
    count, half = stacked.shape[1:]
    stacked = stacked.reshape(place.sources, 2, count, half)
    first = place.sub == 0
    keep = jnp.where(first, stacked[:, 0], stacked[:, 1])
    got = swap(jnp.where(first, stacked[:, 1], stacked[:, 0]), "sub")
    both = jnp.where(first, jnp.concatenate([keep, got], 2), jnp.concatenate([got, keep], 2))
    both = both.reshape(place.sources, count, place.tensors, -1).transpose(0, 2, 1, 3)
    share = lax.psum_scatter(both, "expert", scatter_dimension=0)
    return lax.psum_scatter(share, "tensor", scatter_dimension=0)


def chosen(meta, first_slot):
    rows = meta.shape[1]
    slots = (lax.broadcasted_iota(jnp.int32, (CAP, rows), 0) + first_slot).astype(F32)
    return slots == meta[0:1], slots == meta[1:2]


def place_rows(small, blocks, local, locals_, index_ref, meta_ref, groups, rows_ref):
    width = groups[0].shape[2]
    flat = [group.at[i] for group in groups for i in range(group.shape[0])]
    expert = index_ref[0] * locals_ + local
    for piece, (block, column) in zip(flat, pieces_of(small, blocks, index_ref, width), strict=True):
        one, two = chosen(meta_ref[block], expert * blocks * CAP + block * CAP)
        take = jnp.where(one | two, 1.0, 0.0).astype(BF16)
        start = block * CAP if isinstance(block, int) else pl.multiple_of(block * CAP, 16)
        column = column if isinstance(column, int) else pl.multiple_of(column, 128)
        rows_ref[pl.ds(start, CAP), pl.ds(column, width)] = jnp.dot(
            take, piece[...], preferred_element_type=F32
        ).astype(BF16)


def place_gates(blocks, local, locals_, index_ref, meta_ref, gate_ref):
    expert = index_ref[0] * locals_ + local
    for block in range(blocks):
        meta = meta_ref[block]
        one, two = chosen(meta, expert * blocks * CAP + block * CAP)
        weight = jnp.where(one, meta[2:3], 0.0) + jnp.where(two, meta[3:4], 0.0)
        gate_ref[block * CAP : (block + 1) * CAP, :] = jnp.sum(weight, axis=1, keepdims=True)


def combine_rows(small, blocks, locals_, index_ref, meta_ref, slots_of, outs):
    half = outs[0].shape[1]
    width = half // 2 if small else half
    for out_at, out in enumerate(outs):
        if small:
            expert, sub = index_ref[0], index_ref[1]
            expert_far, sub_far = out_at % 2, out_at // 2
            block = (expert + expert_far - 2 * expert * expert_far) * 2 + sub + sub_far - 2 * sub * sub_far
            start = pl.multiple_of(block * CAP, 16)
        else:
            block = out_at
            start = block * CAP
        total = None
        for local in range(locals_):
            first = (index_ref[0] * locals_ + local) * blocks * CAP + block * CAP
            one, two = chosen(meta_ref[block], first)
            take = jnp.where(one | two, 1.0, 0.0).astype(BF16)
            term = lax.dot_general(
                take, slots_of[local][pl.ds(start, CAP), :], (((0,), (0,)), ((), ())),
                preferred_element_type=F32,
            )
            total = term if total is None else total + term
        total = total.astype(BF16)
        if small:
            low = lax.rem(index_ref[2], 2)
            for chunk in range(2):
                column = (chunk + low - 2 * chunk * low) * width
                out[:, pl.ds(pl.multiple_of(column, 128), width)] = total[:, chunk * width : (chunk + 1) * width]
        else:
            out[...] = total


def first_body(small, blocks, local, locals_, n_groups, index_ref, meta_ref, *refs):
    groups, (gate_w, up_w, out, rows) = refs[:n_groups], refs[n_groups:]

    @pl.when(pl.program_id(0) == 0)
    def _():
        place_rows(small, blocks, local, locals_, index_ref, meta_ref, groups, rows)

    out[0] = jnp.dot(rows[...], gate_w[0], preferred_element_type=F32).astype(BF16)
    out[1] = jnp.dot(rows[...], up_w[0], preferred_element_type=F32).astype(BF16)


def middle_body(small, blocks, local, locals_, n_groups, index_ref, meta_ref, *refs):
    groups, refs = refs[:n_groups], refs[n_groups:]
    last = local == locals_ - 1
    before, refs = (refs[:local], refs[local:]) if last else ((), refs)
    own, other, down, slopes, back, *outs, rows, gates, total, slots = refs
    step = pl.program_id(0)

    @pl.when(step == 0)
    def _():
        place_rows(small, blocks, local, locals_, index_ref, meta_ref, groups, rows)
        place_gates(blocks, local, locals_, index_ref, meta_ref, gates)

    back[...] = nt(rows[...], down[0]).astype(BF16)
    gate_pre = own[0].astype(F32) + other[0].astype(F32)
    up_pre = own[1].astype(F32) + other[1].astype(F32)
    sigmoid = 0.5 * jnp.tanh(0.5 * gate_pre) + 0.5
    weight = gates[...]
    silu = gate_pre * sigmoid
    weighted = up_pre * weight
    hidden = (silu * weighted).astype(BF16)
    slopes[0] = (silu * weight).astype(BF16)
    slopes[1] = (weighted * (sigmoid + silu * (1.0 - sigmoid))).astype(BF16)
    term = jnp.dot(hidden, down[0], preferred_element_type=F32)

    @pl.when(step == 0)
    def _():
        total[...] = term

    @pl.when(step > 0)
    def _():
        total[...] += term

    @pl.when(step == pl.num_programs(0) - 1)
    def _():
        if last:
            slots[...] = total[...].astype(BF16)
            combine_rows(small, blocks, locals_, index_ref, meta_ref, [*before, slots], outs)
        else:
            outs[0][...] = total[...].astype(BF16)


def last_body(small, blocks, local, locals_, index_ref, meta_ref, *refs):
    last = local == locals_ - 1
    before, refs = (refs[:local], refs[local:]) if last else ((), refs)
    own, other, slopes, gate_w, up_w, *outs, total, slots = refs
    step = pl.program_id(0)
    back = own[...].astype(F32) + other[...].astype(F32)
    up_grad = (back * slopes[0].astype(F32)).astype(BF16)
    gate_grad = (back * slopes[1].astype(F32)).astype(BF16)
    term = nt(gate_grad, gate_w[0]) + nt(up_grad, up_w[0])

    @pl.when(step == 0)
    def _():
        total[...] = term

    @pl.when(step > 0)
    def _():
        total[...] += term

    @pl.when(step == pl.num_programs(0) - 1)
    def _():
        if last:
            slots[...] = total[...].astype(BF16)
            combine_rows(small, blocks, locals_, index_ref, meta_ref, [*before, slots], outs)
        else:
            outs[0][...] = total[...].astype(BF16)


def whole_spec(array):
    dims = len(array.shape)
    return pl.BlockSpec(array.shape, lambda f, index: (0,) * dims)


def call(body, grid, index, ins, in_specs, outs, out_specs, scratch, flops, moved):
    return pl.pallas_call(
        body,
        grid_spec=pltpu.PrefetchScalarGridSpec(
            num_scalar_prefetch=1, grid=(grid,), in_specs=in_specs, out_specs=out_specs, scratch_shapes=scratch
        ),
        out_shape=outs,
        compiler_params=pltpu.CompilerParams(vmem_limit_bytes=VMEM_BYTES),
        cost_estimate=pl.CostEstimate(flops=flops, bytes_accessed=moved, transcendentals=0),
    )(index, *ins)


def per_device(tokens, cotangent, expert_ids, gate_values, w_gate, w_up, w_down):
    place = Place()
    small, blocks, index = place.small, place.blocks, place.index
    locals_, half, hidden = w_gate.shape
    count = tokens.shape[0]
    slots = blocks * CAP
    tile = min(1024, hidden)
    steps = hidden // tile
    flops = 2 * slots * half * hidden
    weight_bytes = half * hidden * 2

    block = place.expert * 2 + place.sub
    slot = expert_ids * slots + block * CAP + slot_ranks(expert_ids, EXPERTS)
    meta = jnp.concatenate([slot.astype(F32).T, gate_values.T, jnp.zeros((4, count), F32)])
    meta = lax.all_gather(meta, ("expert", "sub"))

    token_groups = gather_rows(place, tokens)
    grad_groups = gather_rows(place, cotangent)
    n_groups = len(token_groups)

    by_column = [
        pl.BlockSpec((1, half, tile), functools.partial(lambda local, f, index: (local, 0, f), local))
        for local in range(locals_)
    ]
    by_row = [
        pl.BlockSpec((1, tile, half), functools.partial(lambda local, f, index: (local, f, 0), local))
        for local in range(locals_)
    ]
    pair_spec = pl.BlockSpec((2, slots, tile), lambda f, index: (0, 0, f))
    one_spec = pl.BlockSpec((slots, tile), lambda f, index: (0, f))
    pair = jax.ShapeDtypeStruct((2, slots, hidden), BF16)
    one = jax.ShapeDtypeStruct((slots, hidden), BF16)
    slot_rows = jax.ShapeDtypeStruct((slots, half), BF16)
    row_parts = [jax.ShapeDtypeStruct((count, half), BF16)] * blocks

    def ends(local):
        shapes = row_parts if local == locals_ - 1 else [slot_rows]
        return shapes, [whole_spec(shape) for shape in shapes]

    own_pre, other_pre = [], []
    for local in range(locals_):
        own = call(
            functools.partial(first_body, small, blocks, local, locals_, n_groups),
            steps, index,
            [meta, *token_groups, w_gate, w_up],
            [whole_spec(meta), *map(whole_spec, token_groups), by_column[local], by_column[local]],
            pair, pair_spec,
            [pltpu.VMEM((slots, half), BF16)],
            2 * flops, 2 * weight_bytes,
        )
        own_pre.append(own)
        other_pre.append(swap(own, "sub"))

    done, own_back, other_back, slopes = [], [], [], []
    for local in range(locals_):
        before = done if local == locals_ - 1 else []
        shapes, specs = ends(local)
        slope, back, *rest = call(
            functools.partial(middle_body, small, blocks, local, locals_, n_groups),
            steps, index,
            [meta, *grad_groups, *before, own_pre[local], other_pre[local], w_down],
            [whole_spec(meta), *map(whole_spec, grad_groups), *map(whole_spec, before), pair_spec, pair_spec,
             by_row[local]],
            [pair, one, *shapes], [pair_spec, one_spec, *specs],
            [pltpu.VMEM((slots, half), BF16), pltpu.VMEM((slots, 1), F32), pltpu.VMEM((slots, half), F32),
             pltpu.VMEM((slots, half), BF16)],
            2 * flops, weight_bytes,
        )
        slopes.append(slope)
        own_back.append(back)
        other_back.append(swap(back, "sub"))
        done.append(rest[0])
    mixed = scatter_rows(place, rest)

    done = []
    for local in range(locals_):
        before = done if local == locals_ - 1 else []
        shapes, specs = ends(local)
        rest = call(
            functools.partial(last_body, small, blocks, local, locals_),
            steps, index,
            [meta, *before, own_back[local], other_back[local], slopes[local], w_gate, w_up],
            [whole_spec(meta), *map(whole_spec, before), one_spec, one_spec, pair_spec, by_column[local],
             by_column[local]],
            shapes, specs,
            [pltpu.VMEM((slots, half), F32), pltpu.VMEM((slots, half), BF16)],
            2 * flops, 2 * weight_bytes,
        )
        done.append(rest[0])
    return mixed, scatter_rows(place, rest)


def solution(mesh):
    rows = P(("groups", "expert", "sub"), "tensor")
    ids = P(("groups", "expert", "sub"), None)
    return jax.shard_map(
        per_device,
        mesh=mesh,
        in_specs=(rows, rows, ids, ids, P("expert", "sub", "tensor"), P("expert", "sub", "tensor"),
                  P("expert", "tensor", "sub")),
        out_specs=(rows, rows),
        check_vma=False,
    )
```

```python
import functools

import jax
import jax.numpy as jnp
from jax import lax
from jax.experimental import pallas as pl
from jax.experimental.pallas import tpu as pltpu
from jax.sharding import PartitionSpec as P

EXPERTS = 4
CAP = 80
BF16 = jnp.bfloat16
F32 = jnp.float32
VMEM_BYTES = 36 * 1024 * 1024
TILE = 512
DEPTH = 3
COST = 50
FIRST_COST = 1


def swap(value, axis):
    return lax.ppermute(value, axis, [(0, 1), (1, 0)])


def across(value, distance):
    return lax.ppermute(value, "tensor", [(i, i ^ distance) for i in range(lax.axis_size("tensor"))])


def nt(a, b):
    return lax.dot_general(a, b, (((1,), (1,)), ((), ())), preferred_element_type=F32)


class Place:
    def __init__(self):
        self.sources = lax.axis_size("expert")
        self.tensors = lax.axis_size("tensor")
        self.small = self.sources == 2 and self.tensors == 4
        self.expert = lax.axis_index("expert")
        self.sub = lax.axis_index("sub")
        self.tensor = lax.axis_index("tensor")
        self.high = (self.tensor // 2 + self.sub) % 2 == 1
        self.blocks = 2 * self.sources


def other(index, far):
    return index + far - 2 * index * far


def axis_indices():
    return tuple(lax.axis_index(axis) for axis in ("expert", "sub", "tensor"))


def block_at(small, index, place_at):
    if not small:
        return place_at, place_at * CAP
    block = other(index[0], place_at // 2) * 2 + other(index[1], place_at % 2)
    return block, pl.multiple_of(block * CAP, 16)


def far_both(value):
    return lax.ppermute(value, ("expert", "sub"), [(i, 3 - i) for i in range(4)])


def gather_meta(place, meta):
    if place.small:
        return [part[None] for part in (meta, swap(meta, "sub"), swap(meta, "expert"), far_both(meta))]
    return [lax.all_gather(meta, ("expert", "sub"))]


def gather_now(place, rows, after):
    near = [rows] + [across(rows, k) for k in (1, 2, 3)]
    near[3], after = lax.optimization_barrier((near[3], after))
    far = [swap(block, "expert") for block in near]
    low_half = jnp.stack([near[0], near[1], far[0], far[1]])
    high_half = jnp.stack([near[2], near[3], far[2], far[3]])
    keep = jnp.where(place.high, high_half, low_half)
    send = jnp.where(place.high, low_half, high_half)
    return [keep, swap(send, "sub")], [[0, 0, 2, 2], [1, 1, 3, 3]], near[3], after


def gather_first(rows, after):
    rows, _ = lax.optimization_barrier((rows, after))
    return [rows] + [across(rows, k) for k in (1, 2, 3)]


def gather_last(place, near, after):
    *near, _ = lax.optimization_barrier((*near, after))
    low_half, high_half = jnp.stack(near[:2]), jnp.stack(near[2:])
    keep = jnp.where(place.high, high_half, low_half)
    send = jnp.where(place.high, low_half, high_half)
    groups = [keep, swap(send, "sub"), swap(keep, "expert"), far_both(send)]
    return groups, [[0, 0], [1, 1], [2, 2], [3, 3]], [keep, send]


def gather_rows(place, rows):
    count = rows.shape[0]
    whole = lax.all_gather(rows, ("tensor", "expert"))
    whole = whole.reshape(place.tensors, place.sources, count, rows.shape[1])
    whole = whole.transpose(1, 2, 0, 3).reshape(place.sources, count, 2, -1)
    halves = (whole[:, :, 0], whole[:, :, 1])
    first = place.sub == 0
    keep = jnp.where(first, halves[0], halves[1])
    got = swap(jnp.where(first, halves[1], halves[0]), "sub")
    both = jnp.where(first, jnp.stack([keep, got], 1), jnp.stack([got, keep], 1))
    both = both.reshape((2 * place.sources, count, -1))
    return [both], [list(range(2 * place.sources))]


def send_x(place, parts):
    kept, core_near, same_far, core_far = parts
    return kept, swap(core_near, "sub"), swap(same_far, "expert"), far_both(core_far)


def sum_x(place, terms):
    kept, from_core, from_far, from_both = (term.astype(F32) for term in terms)
    own_half, other_half = kept + from_far, from_core + from_both
    return [
        jnp.where(place.high, other_half, own_half).astype(BF16),
        jnp.where(place.high, own_half, other_half).astype(BF16),
    ]


def send_z(near, far, near_next, far_next):
    return near, across(far, 2), across(near_next, 1), across(far_next, 3)


def sum_z(terms):
    return functools.reduce(jnp.add, [term.astype(F32) for term in terms]).astype(BF16)


def scatter_rows(place, parts):
    stacked = jnp.stack(parts)
    count, half = stacked.shape[1:]
    stacked = stacked.reshape(place.sources, 2, count, half)
    first = place.sub == 0
    keep = jnp.where(first, stacked[:, 0], stacked[:, 1])
    got = swap(jnp.where(first, stacked[:, 1], stacked[:, 0]), "sub")
    both = jnp.where(first, jnp.concatenate([keep, got], 2), jnp.concatenate([got, keep], 2))
    both = both.reshape(place.sources, count, place.tensors, -1).transpose(0, 2, 1, 3)
    share = lax.psum_scatter(both, "expert", scatter_dimension=0)
    return lax.psum_scatter(share, "tensor", scatter_dimension=0)


def route_rows(small, locals_, index, metas, take_ref, gate_ref):
    places = [ref.at[i] for ref in metas for i in range(ref.shape[0])]
    rows = places[0].shape[0]
    row, column = (lax.broadcasted_iota(jnp.int32, (rows, rows), axis) for axis in (0, 1))
    before = jnp.where(row < column, 1.0, 0.0).astype(BF16)
    slot = lax.broadcasted_iota(jnp.int32, (CAP, rows), 0).astype(F32)
    for place_at, meta_ref in enumerate(places):
        start = block_at(small, index, place_at)[1]
        meta = jnp.concatenate([meta_ref[...], jnp.zeros((rows, 128 - meta_ref.shape[1]), F32)], axis=1).T
        for local in range(locals_):
            number = (index[0] * locals_ + local).astype(F32)
            one, two = meta[0:1] == number, meta[1:2] == number
            named = jnp.where(one | two, 1.0, 0.0)
            rank = jnp.dot(
                jnp.broadcast_to(named, (16, rows)).astype(BF16), before, preferred_element_type=F32
            )
            take = jnp.where(jnp.where(one | two, rank[0:1], -1.0) == slot, 1.0, 0.0)
            gate = jnp.where(one, meta[2:3], 0.0) + jnp.where(two, meta[3:4], 0.0)
            take_ref[local, place_at] = take.astype(BF16)
            gate_ref[local, pl.ds(start, CAP), :] = jnp.sum(take * gate, axis=1, keepdims=True)


def place_rows(small, index, take_ref, local, groups, places, rows_ref):
    width = groups[0].shape[2]
    seen = {}
    for group, held in zip(groups, places, strict=True):
        for i, place_at in enumerate(held):
            chunk = seen[place_at] = seen.get(place_at, -1) + 1
            start = block_at(small, index, place_at)[1]
            column = pl.multiple_of(other(lax.rem(index[2], 2), chunk) * width, 128) if small else 0
            rows_ref[pl.ds(start, CAP), pl.ds(column, width)] = jnp.dot(
                take_ref[local, place_at], group[i], preferred_element_type=F32
            ).astype(BF16)


def combine_rows(small, index, take_ref, slots_of, outs):
    half, width = slots_of[0].shape[1], outs[0].shape[1]
    chunks = 2 if small else 1
    places = len(outs) * width // half
    for place_at in range(places):
        start = block_at(small, index, place_at)[1]
        for chunk in range(chunks):
            span = half // chunks
            column = pl.multiple_of(other(lax.rem(index[2], 2), chunk) * span, 128) if small else 0
            total = None
            for local, slots in enumerate(slots_of):
                term = lax.dot_general(
                    take_ref[local, place_at], slots[pl.ds(start, CAP), pl.ds(column, span)],
                    (((0,), (0,)), ((), ())), preferred_element_type=F32,
                )
                total = term if total is None else total + term
            if width == half:
                outs[place_at][:, chunk * span : (chunk + 1) * span] = total.astype(BF16)
            else:
                outs[chunk * places + place_at][...] = total.astype(BF16)


class Stream:
    def __init__(self, weights, at, tile, rings, sems):
        self.weights, self.at, self.tile, self.rings, self.sems = weights, at, tile, rings, sems
        self.depth = rings[0].shape[0]

    def copies(self, step):
        slot = lax.rem(step, self.depth)
        cut = pl.ds(pl.multiple_of(step * self.tile, self.tile), self.tile)
        return [
            pltpu.make_async_copy(weight.at[self.at(cut)], ring.at[slot], self.sems.at[i, slot])
            for i, (weight, ring) in enumerate(zip(self.weights, self.rings, strict=True))
        ]

    def start(self, steps):
        for step in range(min(self.depth - 1, steps)):
            for copy in self.copies(step):
                copy.start()

    def take(self, step):
        @pl.when(step + self.depth - 1 < pl.num_programs(0))
        def _():
            for copy in self.copies(step + self.depth - 1):
                copy.start()

        for copy in self.copies(step):
            copy.wait()
        return [ring.at[lax.rem(step, self.depth)] for ring in self.rings]


def first_body(small, local, locals_, places, n_routes, n_after, tile, steps, *refs):
    routes, refs = refs[:n_routes], refs[n_routes + n_after :]
    groups, (gate_w, up_w, out, *routed, rows, gate_ring, up_ring, sems) = refs[: len(places)], refs[len(places) :]
    take_ref = routes[0] if local else routed[0]
    stream = Stream([gate_w, up_w], lambda cut: (local, slice(None), cut), tile, [gate_ring, up_ring], sems)
    step = pl.program_id(0)

    @pl.when(step == 0)
    def _():
        stream.start(steps)
        if not local:
            route_rows(small, locals_, axis_indices(), routes, *routed)
        place_rows(small, axis_indices(), take_ref, local, groups, places, rows)

    for i, weight in enumerate(stream.take(step)):
        out[i] = jnp.dot(rows[...], weight[...], preferred_element_type=F32).astype(BF16)


def middle_body(small, local, locals_, places, tile, steps, take_ref, gate_ref, *refs):
    groups, refs = refs[: len(places)], refs[len(places) :]
    last = local == locals_ - 1
    before, refs = (refs[:local], refs[local:]) if last else ((), refs)
    own, got, down, slopes, back, *outs, rows, total, slots, ring, sems = refs
    stream = Stream([down], lambda cut: (local, cut), tile, [ring], sems)
    step = pl.program_id(0)

    @pl.when(step == 0)
    def _():
        stream.start(steps)
        place_rows(small, axis_indices(), take_ref, local, groups, places, rows)
        total[...] = jnp.zeros_like(total)

    (weight,) = stream.take(step)
    back[...] = nt(rows[...], weight[...]).astype(BF16)
    gate_pre = own[0].astype(F32) + got[0].astype(F32)
    up_pre = own[1].astype(F32) + got[1].astype(F32)
    sigmoid = 0.5 * jnp.tanh(0.5 * gate_pre) + 0.5
    silu = gate_pre * sigmoid
    hidden = (silu * up_pre).astype(BF16)
    slopes[0] = silu.astype(BF16)
    slopes[1] = (up_pre * (sigmoid + silu * (1.0 - sigmoid))).astype(BF16)
    total[...] += jnp.dot(hidden, weight[...], preferred_element_type=F32)

    @pl.when(step == pl.num_programs(0) - 1)
    def _():
        finish(small, last, take_ref, gate_ref[local], before, total, slots, outs)


def last_body(small, local, locals_, n_after, tile, steps, take_ref, gate_ref, *refs):
    refs = refs[n_after:]
    last = local == locals_ - 1
    before, refs = (refs[:local], refs[local:]) if last else ((), refs)
    own, got, slopes, gate_w, up_w, *outs, total, slots, gate_ring, up_ring, sems = refs
    stream = Stream([gate_w, up_w], lambda cut: (local, slice(None), cut), tile, [gate_ring, up_ring], sems)
    step = pl.program_id(0)

    @pl.when(step == 0)
    def _():
        stream.start(steps)
        total[...] = jnp.zeros_like(total)

    gate_tile, up_tile = stream.take(step)
    back = own[...].astype(F32) + got[...].astype(F32)
    up_grad = (back * slopes[0].astype(F32)).astype(BF16)
    gate_grad = (back * slopes[1].astype(F32)).astype(BF16)
    total[...] += nt(gate_grad, gate_tile[...]) + nt(up_grad, up_tile[...])

    @pl.when(step == pl.num_programs(0) - 1)
    def _():
        finish(small, last, take_ref, gate_ref[local], before, total, slots, outs)


def finish(small, last, take_ref, gate, before, total, slots, outs):
    weighted = (total[...] * gate).astype(BF16)
    if last:
        slots[...] = weighted
        combine_rows(small, axis_indices(), take_ref, [*before, slots], outs)
    else:
        outs[0][...] = weighted


def whole(array):
    dims = len(array.shape)
    return pl.BlockSpec(array.shape, lambda f: (0,) * dims)


def call(body, steps, routes, after, near, near_specs, weights, outs, out_specs, scratch, flops):
    anywhere = pl.BlockSpec(memory_space=pl.ANY)
    return pl.pallas_call(
        body,
        grid=(steps,),
        in_specs=[*map(whole, routes), *[anywhere] * len(after), *near_specs,
                  *[anywhere] * len(weights)],
        out_specs=out_specs,
        out_shape=outs,
        scratch_shapes=scratch,
        compiler_params=pltpu.CompilerParams(vmem_limit_bytes=VMEM_BYTES),
        cost_estimate=pl.CostEstimate(flops=flops, bytes_accessed=0, transcendentals=0),
    )(*routes, *after, *near, *weights)


def per_device(tokens, cotangent, expert_ids, gate_values, w_gate, w_up, w_down):
    place = Place()
    small, blocks = place.small, place.blocks
    locals_, half, hidden = w_gate.shape
    count = tokens.shape[0]
    slots = blocks * CAP
    flops = 2 * slots * half * hidden

    ids = jnp.pad(expert_ids.astype(F32), ((0, 0), (0, gate_values.shape[1])))
    metas = gather_meta(place, ids + jnp.pad(gate_values, ((0, 0), (expert_ids.shape[1], 0))))
    routed = [jax.ShapeDtypeStruct((locals_, blocks, CAP, count), BF16),
              jax.ShapeDtypeStruct((locals_, slots, 1), F32)]

    if small:
        token_groups, token_places, token_last, metas = gather_now(place, tokens, metas)
        grad_near = gather_first(cotangent, token_last)
    else:
        token_groups, token_places = gather_rows(place, tokens)
        grad_groups, grad_places = gather_rows(place, cotangent)

    tile = min(TILE, hidden)
    steps = hidden // tile
    pair = pltpu.HBM((2, slots, hidden), BF16)
    one = pltpu.HBM((slots, hidden), BF16)
    pair_spec = pl.BlockSpec((2, slots, tile), lambda f: (0, 0, f))
    one_spec = pl.BlockSpec((slots, tile), lambda f: (0, f))
    two_sems, one_sem = pltpu.SemaphoreType.DMA((2, DEPTH)), pltpu.SemaphoreType.DMA((1, DEPTH))

    def ends(local, width):
        return [jax.ShapeDtypeStruct((count, width), BF16)] * (blocks * half // width) if local == locals_ - 1 else [
            jax.ShapeDtypeStruct((slots, width), BF16)]

    own_pre, got_pre, after = [], [], []
    for local in range(locals_):
        ring = pltpu.VMEM((DEPTH, half, tile), BF16)
        routes, new = ([take], []) if local else (metas, routed)
        own, *new = call(
            functools.partial(first_body, small, local, locals_, token_places, len(routes), len(after), tile, steps),
            steps, routes, after, token_groups, [*map(whole, token_groups)], [w_gate, w_up],
            [pair, *new], [pair_spec, *map(whole, new)], [pltpu.VMEM((slots, half), BF16), ring, ring, two_sems],
            (COST if local else FIRST_COST) * flops,
        )
        if not local:
            take, gate = new
        own_pre.append(own)
        got_pre.append(swap(own, "sub"))
        if small and local == 0:
            grad_groups, grad_places, after = gather_last(place, grad_near, own)

    done, own_back, got_back, slopes = [], [], [], []
    for local in range(locals_):
        before = done if local == locals_ - 1 else []
        outs = ends(local, half)
        slope, back, *mixed_parts = call(
            functools.partial(middle_body, small, local, locals_, grad_places, tile, steps),
            steps, [take, gate], [], [*grad_groups, *before, own_pre[local], got_pre[local]],
            [*map(whole, [*grad_groups, *before]), pair_spec, pair_spec], [w_down],
            [pair, one, *outs], [pair_spec, one_spec, *map(whole, outs)],
            [pltpu.VMEM((slots, half), BF16), pltpu.VMEM((slots, half), F32), pltpu.VMEM((slots, half), BF16),
             pltpu.VMEM((DEPTH, tile, half), BF16), one_sem],
            COST * flops,
        )
        slopes.append(slope)
        own_back.append(back)
        got_back.append(swap(back, "sub"))
        done.append(mixed_parts[0])

    ring = pltpu.VMEM((DEPTH, half, tile), BF16)
    done, after = [], []
    mixed_terms = send_x(place, mixed_parts) if small else []
    for local in range(locals_):
        last = local == locals_ - 1
        before = done if last else []
        outs = ends(local, half // 2 if small and last else half)
        grad_parts = call(
            functools.partial(last_body, small, local, locals_, len(after), tile, steps),
            steps, [take, gate], after, [*before, own_back[local], got_back[local], slopes[local]],
            [*map(whole, before), one_spec, one_spec, pair_spec], [w_gate, w_up],
            outs, [*map(whole, outs)],
            [pltpu.VMEM((slots, half), F32), pltpu.VMEM((slots, half), BF16), ring, ring, two_sems],
            COST * flops,
        )
        done.append(grad_parts[0])
        if small and local == 0:
            *terms, _ = lax.optimization_barrier((*mixed_terms, grad_parts[0]))
            terms = [[term[:, i * half // 2 : (i + 1) * half // 2] for term in terms] for i in range(2)]
            after = [*sum_x(place, terms[0]), *sum_x(place, terms[1])]
            mixed_terms = send_z(*after)
    if not small:
        return scatter_rows(place, mixed_parts), scatter_rows(place, grad_parts)
    *mixed_terms, grad_parts = lax.optimization_barrier((*mixed_terms, grad_parts))
    next_terms = send_x(place, grad_parts[blocks:])
    last_terms = send_x(place, grad_parts[:blocks])
    return sum_z(mixed_terms), sum_z(send_z(*sum_x(place, last_terms), *sum_x(place, next_terms)))


def solution(mesh):
    rows = P(("groups", "expert", "sub"), "tensor")
    ids = P(("groups", "expert", "sub"), None)
    return jax.shard_map(
        per_device,
        mesh=mesh,
        in_specs=(rows, rows, ids, ids, P("expert", "sub", "tensor"), P("expert", "sub", "tensor"),
                  P("expert", "tensor", "sub")),
        out_specs=(rows, rows),
        check_vma=False,
    )
```

```python
import functools

import jax
import jax.numpy as jnp
from jax import lax
from jax.experimental import pallas as pl
from jax.experimental.pallas import tpu as pltpu
from jax.sharding import PartitionSpec as P

EXPERTS = 4
CAP = 80
BF16 = jnp.bfloat16
F32 = jnp.float32
VMEM_BYTES = 36 * 1024 * 1024
TILE = 512
DEPTH = 3
COST = 50
FIRST_COST = 0


def swap(value, axis):
    return lax.ppermute(value, axis, [(0, 1), (1, 0)])


def across(value, distance):
    return lax.ppermute(value, "tensor", [(i, i ^ distance) for i in range(lax.axis_size("tensor"))])


def nt(a, b):
    return lax.dot_general(a, b, (((1,), (1,)), ((), ())), preferred_element_type=F32)


class Place:
    def __init__(self):
        self.sources = lax.axis_size("expert")
        self.tensors = lax.axis_size("tensor")
        self.small = self.sources == 2 and self.tensors == 4
        self.expert = lax.axis_index("expert")
        self.sub = lax.axis_index("sub")
        self.tensor = lax.axis_index("tensor")
        self.high = (self.tensor // 2 + self.sub) % 2 == 1
        self.blocks = 2 * self.sources


def other(index, far):
    return index + far - 2 * index * far


def axis_indices():
    return tuple(lax.axis_index(axis) for axis in ("expert", "sub", "tensor"))


def block_at(small, index, place_at):
    if not small:
        return place_at, place_at * CAP
    block = other(index[0], place_at // 2) * 2 + other(index[1], place_at % 2)
    return block, pl.multiple_of(block * CAP, 16)


def far_both(value):
    return lax.ppermute(value, ("expert", "sub"), [(i, 3 - i) for i in range(4)])


def gather_meta(place, meta):
    if place.small:
        pair = jnp.stack([meta, swap(meta, "sub")])
        return jnp.concatenate([pair, swap(pair, "expert")])
    return lax.all_gather(meta, ("expert", "sub"))


def gather_now(place, rows, meta):
    near = [rows] + [across(rows, k) for k in (1, 2, 3)]
    near[3], meta = lax.optimization_barrier((near[3], meta))
    far = [swap(block, "expert") for block in near]
    low_half = jnp.stack([near[0], near[1], far[0], far[1]])
    high_half = jnp.stack([near[2], near[3], far[2], far[3]])
    keep = jnp.where(place.high, high_half, low_half)
    send = jnp.where(place.high, low_half, high_half)
    return [keep, swap(send, "sub")], [[0, 0, 2, 2], [1, 1, 3, 3]], near[3], meta


def gather_first(rows, after):
    rows, _ = lax.optimization_barrier((rows, after))
    return [rows] + [across(rows, k) for k in (1, 2, 3)]


def gather_last(place, near, after):
    *near, _ = lax.optimization_barrier((*near, after))
    low_half, high_half = jnp.stack(near[:2]), jnp.stack(near[2:])
    keep = jnp.where(place.high, high_half, low_half)
    send = jnp.where(place.high, low_half, high_half)
    groups = [keep, swap(send, "sub"), swap(keep, "expert"), far_both(send)]
    return groups, [[0, 0], [1, 1], [2, 2], [3, 3]], [keep, send]


def gather_rows(place, rows):
    count = rows.shape[0]
    whole = lax.all_gather(rows, ("tensor", "expert"))
    whole = whole.reshape(place.tensors, place.sources, count, rows.shape[1])
    whole = whole.transpose(1, 2, 0, 3).reshape(place.sources, count, 2, -1)
    halves = (whole[:, :, 0], whole[:, :, 1])
    first = place.sub == 0
    keep = jnp.where(first, halves[0], halves[1])
    got = swap(jnp.where(first, halves[1], halves[0]), "sub")
    both = jnp.where(first, jnp.stack([keep, got], 1), jnp.stack([got, keep], 1))
    both = both.reshape((2 * place.sources, count, -1))
    return [both], [list(range(2 * place.sources))]


def send_x(place, parts):
    kept, core_near, same_far, core_far = parts
    return kept, swap(core_near, "sub"), swap(same_far, "expert"), far_both(core_far)


def sum_x(place, terms):
    kept, from_core, from_far, from_both = (term.astype(F32) for term in terms)
    own_half, other_half = kept + from_far, from_core + from_both
    return [
        jnp.where(place.high, other_half, own_half).astype(BF16),
        jnp.where(place.high, own_half, other_half).astype(BF16),
    ]


def send_z(near, far, near_next, far_next):
    return near, across(far, 2), across(near_next, 1), across(far_next, 3)


def sum_z(terms):
    return functools.reduce(jnp.add, [term.astype(F32) for term in terms]).astype(BF16)


def scatter_rows(place, parts):
    stacked = jnp.stack(parts)
    count, half = stacked.shape[1:]
    stacked = stacked.reshape(place.sources, 2, count, half)
    first = place.sub == 0
    keep = jnp.where(first, stacked[:, 0], stacked[:, 1])
    got = swap(jnp.where(first, stacked[:, 1], stacked[:, 0]), "sub")
    both = jnp.where(first, jnp.concatenate([keep, got], 2), jnp.concatenate([got, keep], 2))
    both = both.reshape(place.sources, count, place.tensors, -1).transpose(0, 2, 1, 3)
    share = lax.psum_scatter(both, "expert", scatter_dimension=0)
    return lax.psum_scatter(share, "tensor", scatter_dimension=0)


def route_rows(small, locals_, index, meta_ref, take_ref, gate_ref):
    rows = meta_ref.shape[2]
    row, column = (lax.broadcasted_iota(jnp.int32, (rows, rows), axis) for axis in (0, 1))
    before = jnp.where(row < column, 1.0, 0.0).astype(BF16)
    slot = lax.broadcasted_iota(jnp.int32, (CAP, rows), 0).astype(F32)
    for place_at in range(meta_ref.shape[0]):
        start = block_at(small, index, place_at)[1]
        meta = meta_ref[place_at]
        for local in range(locals_):
            number = (index[0] * locals_ + local).astype(F32)
            one, two = meta[0:1] == number, meta[1:2] == number
            named = jnp.where(one | two, 1.0, 0.0)
            rank = jnp.dot(
                jnp.broadcast_to(named, (16, rows)).astype(BF16), before, preferred_element_type=F32
            )
            take = jnp.where(jnp.where(one | two, rank[0:1], -1.0) == slot, 1.0, 0.0)
            gate = jnp.where(one, meta[2:3], 0.0) + jnp.where(two, meta[3:4], 0.0)
            take_ref[local, place_at] = take.astype(BF16)
            gate_ref[local, pl.ds(start, CAP), :] = jnp.sum(take * gate, axis=1, keepdims=True)


def place_rows(small, index, take_ref, local, groups, places, rows_ref):
    width = groups[0].shape[2]
    seen = {}
    for group, held in zip(groups, places, strict=True):
        for i, place_at in enumerate(held):
            chunk = seen[place_at] = seen.get(place_at, -1) + 1
            start = block_at(small, index, place_at)[1]
            column = pl.multiple_of(other(lax.rem(index[2], 2), chunk) * width, 128) if small else 0
            rows_ref[pl.ds(start, CAP), pl.ds(column, width)] = jnp.dot(
                take_ref[local, place_at], group[i], preferred_element_type=F32
            ).astype(BF16)


def combine_rows(small, index, take_ref, slots_of, outs):
    half, width = slots_of[0].shape[1], outs[0].shape[1]
    chunks = 2 if small else 1
    places = len(outs) * width // half
    for place_at in range(places):
        start = block_at(small, index, place_at)[1]
        for chunk in range(chunks):
            span = half // chunks
            column = pl.multiple_of(other(lax.rem(index[2], 2), chunk) * span, 128) if small else 0
            total = None
            for local, slots in enumerate(slots_of):
                term = lax.dot_general(
                    take_ref[local, place_at], slots[pl.ds(start, CAP), pl.ds(column, span)],
                    (((0,), (0,)), ((), ())), preferred_element_type=F32,
                )
                total = term if total is None else total + term
            if width == half:
                outs[place_at][:, chunk * span : (chunk + 1) * span] = total.astype(BF16)
            else:
                outs[chunk * places + place_at][...] = total.astype(BF16)


class Stream:
    def __init__(self, arrays, places, tile, rings, sems):
        self.arrays, self.places, self.tile, self.rings, self.sems = arrays, places, tile, rings, sems
        self.depth = rings[0].shape[0]

    def copies(self, step):
        slot = lax.rem(step, self.depth)
        cut = pl.ds(pl.multiple_of(step * self.tile, self.tile), self.tile)
        return [
            pltpu.make_async_copy(array.at[place(cut)], ring.at[slot], self.sems.at[i, slot])
            for i, (array, place, ring) in enumerate(zip(self.arrays, self.places, self.rings, strict=True))
        ]

    def start(self, steps):
        for step in range(min(self.depth - 1, steps)):
            for copy in self.copies(step):
                copy.start()

    def take(self, step):
        @pl.when(step + self.depth - 1 < pl.num_programs(0))
        def _():
            for copy in self.copies(step + self.depth - 1):
                copy.start()

        for copy in self.copies(step):
            copy.wait()
        return [ring.at[lax.rem(step, self.depth)] for ring in self.rings]


def column_tile(local):
    return lambda cut: (local, slice(None), cut)


def pair_tile(cut):
    return slice(None), slice(None), cut


def one_tile(cut):
    return slice(None), cut


def first_body(small, local, locals_, places, n_routes, n_after, tile, steps, *refs):
    routes, refs = refs[:n_routes], refs[n_routes + n_after :]
    groups, (gate_w, up_w, out, *routed, rows, gate_ring, up_ring, sems) = refs[: len(places)], refs[len(places) :]
    take_ref = routes[0] if local else routed[0]
    stream = Stream([gate_w, up_w], [column_tile(local)] * 2, tile, [gate_ring, up_ring], sems)
    step = pl.program_id(0)

    @pl.when(step == 0)
    def _():
        stream.start(steps)
        if not local:
            route_rows(small, locals_, axis_indices(), *routes, *routed)
        place_rows(small, axis_indices(), take_ref, local, groups, places, rows)

    for i, weight in enumerate(stream.take(step)):
        out[i] = jnp.dot(rows[...], weight[...], preferred_element_type=F32).astype(BF16)


def middle_body(small, local, locals_, places, tile, steps, take_ref, gate_ref, *refs):
    groups, refs = refs[: len(places)], refs[len(places) :]
    last = local == locals_ - 1
    before, refs = (refs[:local], refs[local:]) if last else ((), refs)
    own_at, got_at, down, slopes, back, *outs, rows, total, slots, own_ring, got_ring, ring, sems = refs
    stream = Stream(
        [down, own_at, got_at], [lambda cut: (local, cut), pair_tile, pair_tile], tile, [ring, own_ring, got_ring], sems
    )
    step = pl.program_id(0)

    @pl.when(step == 0)
    def _():
        stream.start(steps)
        place_rows(small, axis_indices(), take_ref, local, groups, places, rows)
        total[...] = jnp.zeros_like(total)

    weight, own, got = stream.take(step)
    back[...] = nt(rows[...], weight[...]).astype(BF16)
    gate_pre = own[0].astype(F32) + got[0].astype(F32)
    up_pre = own[1].astype(F32) + got[1].astype(F32)
    sigmoid = 0.5 * jnp.tanh(0.5 * gate_pre) + 0.5
    silu = gate_pre * sigmoid
    hidden = (silu * up_pre).astype(BF16)
    slopes[0] = silu.astype(BF16)
    slopes[1] = (up_pre * (sigmoid + silu * (1.0 - sigmoid))).astype(BF16)
    total[...] += jnp.dot(hidden, weight[...], preferred_element_type=F32)

    @pl.when(step == pl.num_programs(0) - 1)
    def _():
        finish(small, last, take_ref, gate_ref[local], before, total, slots, outs)


def last_body(small, local, locals_, n_after, tile, steps, take_ref, gate_ref, *refs):
    refs = refs[n_after:]
    last = local == locals_ - 1
    before, refs = (refs[:local], refs[local:]) if last else ((), refs)
    own_at, got_at, slopes_at, gate_w, up_w, *outs, total, slots, own_ring, got_ring, slope_ring, gate_ring, up_ring, sems = refs
    stream = Stream(
        [own_at, got_at, slopes_at, gate_w, up_w], [one_tile, one_tile, pair_tile, *[column_tile(local)] * 2], tile,
        [own_ring, got_ring, slope_ring, gate_ring, up_ring], sems,
    )
    step = pl.program_id(0)

    @pl.when(step == 0)
    def _():
        stream.start(steps)
        total[...] = jnp.zeros_like(total)

    own, got, slopes, gate_tile, up_tile = stream.take(step)
    back = own[...].astype(F32) + got[...].astype(F32)
    up_grad = (back * slopes[0].astype(F32)).astype(BF16)
    gate_grad = (back * slopes[1].astype(F32)).astype(BF16)
    total[...] += nt(gate_grad, gate_tile[...]) + nt(up_grad, up_tile[...])

    @pl.when(step == pl.num_programs(0) - 1)
    def _():
        finish(small, last, take_ref, gate_ref[local], before, total, slots, outs)


def finish(small, last, take_ref, gate, before, total, slots, outs):
    weighted = (total[...] * gate).astype(BF16)
    if last:
        slots[...] = weighted
        combine_rows(small, axis_indices(), take_ref, [*before, slots], outs)
    else:
        outs[0][...] = weighted


def whole(array):
    dims = len(array.shape)
    return pl.BlockSpec(array.shape, lambda f: (0,) * dims)


def call(body, steps, routes, after, near, near_specs, weights, outs, out_specs, scratch, flops):
    anywhere = pl.BlockSpec(memory_space=pl.ANY)
    return pl.pallas_call(
        body,
        grid=(steps,),
        in_specs=[*map(whole, routes), *[anywhere] * len(after), *near_specs,
                  *[anywhere] * len(weights)],
        out_specs=out_specs,
        out_shape=outs,
        scratch_shapes=scratch,
        compiler_params=pltpu.CompilerParams(vmem_limit_bytes=VMEM_BYTES),
        cost_estimate=pl.CostEstimate(flops=flops, bytes_accessed=0, transcendentals=0),
    )(*routes, *after, *near, *weights)


def in_hbm(*arrays):
    return [pltpu.with_memory_space_constraint(array, pltpu.HBM) for array in arrays]


def per_device(tokens, cotangent, expert_ids, gate_values, w_gate, w_up, w_down):
    place = Place()
    small, blocks = place.small, place.blocks
    locals_, half, hidden = w_gate.shape
    count = tokens.shape[0]
    slots = blocks * CAP
    flops = 2 * slots * half * hidden

    meta = jnp.concatenate([expert_ids.astype(F32).T, gate_values.T, jnp.zeros((4, count), F32)])
    meta = gather_meta(place, meta)
    routed = [jax.ShapeDtypeStruct((locals_, blocks, CAP, count), BF16),
              jax.ShapeDtypeStruct((locals_, slots, 1), F32)]

    if small:
        token_groups, token_places, token_last, meta = gather_now(place, tokens, meta)
        grad_near = gather_first(cotangent, token_last)
    else:
        token_groups, token_places = gather_rows(place, tokens)
        grad_groups, grad_places = gather_rows(place, cotangent)

    tile = min(TILE, hidden)
    steps = hidden // tile
    pair = pltpu.HBM((2, slots, hidden), BF16)
    one = pltpu.HBM((slots, hidden), BF16)
    pair_spec = pl.BlockSpec((2, slots, tile), lambda f: (0, 0, f))
    one_spec = pl.BlockSpec((slots, tile), lambda f: (0, f))
    pair_ring, one_ring = pltpu.VMEM((DEPTH, 2, slots, tile), BF16), pltpu.VMEM((DEPTH, slots, tile), BF16)

    def sems(arrays):
        return pltpu.SemaphoreType.DMA((arrays, DEPTH))


    def ends(local, width):
        return [jax.ShapeDtypeStruct((count, width), BF16)] * (blocks * half // width) if local == locals_ - 1 else [
            jax.ShapeDtypeStruct((slots, width), BF16)]

    own_pre, got_pre, after = [], [], []
    for local in range(locals_):
        ring = pltpu.VMEM((DEPTH, half, tile), BF16)
        routes, new = ([take], []) if local else ([meta], routed)
        own, *new = call(
            functools.partial(first_body, small, local, locals_, token_places, len(routes), len(after), tile, steps),
            steps, routes, after, token_groups, [*map(whole, token_groups)], [w_gate, w_up],
            [pair, *new], [pair_spec, *map(whole, new)], [pltpu.VMEM((slots, half), BF16), ring, ring, sems(2)],
            (COST if local else FIRST_COST) * flops,
        )
        if not local:
            take, gate = new
        own_pre.append(own)
        got_pre.append(swap(own, "sub"))
        if small and local == 0:
            grad_groups, grad_places, after = gather_last(place, grad_near, own)

    done, own_back, got_back, slopes = [], [], [], []
    for local in range(locals_):
        before = done if local == locals_ - 1 else []
        outs = ends(local, half)
        slope, back, *mixed_parts = call(
            functools.partial(middle_body, small, local, locals_, grad_places, tile, steps),
            steps, [take, gate], [], [*grad_groups, *before], [*map(whole, [*grad_groups, *before])],
            [*in_hbm(own_pre[local], got_pre[local]), w_down],
            [pair, one, *outs], [pair_spec, one_spec, *map(whole, outs)],
            [pltpu.VMEM((slots, half), BF16), pltpu.VMEM((slots, half), F32), pltpu.VMEM((slots, half), BF16),
             pair_ring, pair_ring, pltpu.VMEM((DEPTH, tile, half), BF16), sems(3)],
            COST * flops,
        )
        slopes.append(slope)
        own_back.append(back)
        got_back.append(swap(back, "sub"))
        done.append(mixed_parts[0])

    ring = pltpu.VMEM((DEPTH, half, tile), BF16)
    done, after = [], []
    mixed_terms = send_x(place, mixed_parts) if small else []
    for local in range(locals_):
        last = local == locals_ - 1
        before = done if last else []
        outs = ends(local, half // 2 if small and last else half)
        grad_parts = call(
            functools.partial(last_body, small, local, locals_, len(after), tile, steps),
            steps, [take, gate], after, before, [*map(whole, before)],
            [*in_hbm(own_back[local], got_back[local], slopes[local]), w_gate, w_up],
            outs, [*map(whole, outs)],
            [pltpu.VMEM((slots, half), F32), pltpu.VMEM((slots, half), BF16), one_ring, one_ring, pair_ring, ring, ring,
             sems(5)],
            COST * flops,
        )
        done.append(grad_parts[0])
        if small and local == 0:
            *terms, _ = lax.optimization_barrier((*mixed_terms, grad_parts[0]))
            terms = [[term[:, i * half // 2 : (i + 1) * half // 2] for term in terms] for i in range(2)]
            after = [*sum_x(place, terms[0]), *sum_x(place, terms[1])]
            mixed_terms = send_z(*after)
    if not small:
        return scatter_rows(place, mixed_parts), scatter_rows(place, grad_parts)
    *mixed_terms, grad_parts = lax.optimization_barrier((*mixed_terms, grad_parts))
    next_terms = send_x(place, grad_parts[blocks:])
    last_terms = send_x(place, grad_parts[:blocks])
    return sum_z(mixed_terms), sum_z(send_z(*sum_x(place, last_terms), *sum_x(place, next_terms)))


def solution(mesh):
    rows = P(("groups", "expert", "sub"), "tensor")
    ids = P(("groups", "expert", "sub"), None)
    return jax.shard_map(
        per_device,
        mesh=mesh,
        in_specs=(rows, rows, ids, ids, P("expert", "sub", "tensor"), P("expert", "sub", "tensor"),
                  P("expert", "tensor", "sub")),
        out_specs=(rows, rows),
        check_vma=False,
    )
```

```python
import functools

import jax
import jax.numpy as jnp
from jax import lax
from jax.experimental import pallas as pl
from jax.experimental.pallas import tpu as pltpu
from jax.sharding import PartitionSpec as P

EXPERTS = 4
CAP = 80
BF16 = jnp.bfloat16
F32 = jnp.float32
VMEM_BYTES = 36 * 1024 * 1024
TILE = 512
DEPTH = 3
COST = 50
FIRST_COST = 1000


def swap(value, axis):
    return lax.ppermute(value, axis, [(0, 1), (1, 0)])


def across(value, distance):
    return lax.ppermute(value, "tensor", [(i, i ^ distance) for i in range(lax.axis_size("tensor"))])


def nt(a, b):
    return lax.dot_general(a, b, (((1,), (1,)), ((), ())), preferred_element_type=F32)


class Place:
    def __init__(self):
        self.sources = lax.axis_size("expert")
        self.tensors = lax.axis_size("tensor")
        self.small = self.sources == 2 and self.tensors == 4
        self.expert = lax.axis_index("expert")
        self.sub = lax.axis_index("sub")
        self.tensor = lax.axis_index("tensor")
        self.high = (self.tensor // 2 + self.sub) % 2 == 1
        self.blocks = 2 * self.sources


def other(index, far):
    return index + far - 2 * index * far


def axis_indices():
    return tuple(lax.axis_index(axis) for axis in ("expert", "sub", "tensor"))


def block_at(small, index, place_at):
    if not small:
        return place_at, place_at * CAP
    block = other(index[0], place_at // 2) * 2 + other(index[1], place_at % 2)
    return block, pl.multiple_of(block * CAP, 16)


def far_both(value):
    return lax.ppermute(value, ("expert", "sub"), [(i, 3 - i) for i in range(4)])


def gather_meta(place, meta):
    if place.small:
        pair = jnp.stack([meta, swap(meta, "sub")])
        return jnp.concatenate([pair, swap(pair, "expert")])
    return lax.all_gather(meta, ("expert", "sub"))


def gather_now(place, rows, meta):
    near = [rows] + [across(rows, k) for k in (1, 2, 3)]
    near[3], meta = lax.optimization_barrier((near[3], meta))
    far = [swap(block, "expert") for block in near]
    low_half = jnp.stack([near[0], near[1], far[0], far[1]])
    high_half = jnp.stack([near[2], near[3], far[2], far[3]])
    keep = jnp.where(place.high, high_half, low_half)
    send = jnp.where(place.high, low_half, high_half)
    return [keep, swap(send, "sub")], [[0, 0, 2, 2], [1, 1, 3, 3]], near[3], meta


def gather_first(rows, after):
    rows, _ = lax.optimization_barrier((rows, after))
    return [rows] + [across(rows, k) for k in (1, 2, 3)]


def gather_last(place, near, after):
    *near, _ = lax.optimization_barrier((*near, after))
    low_half, high_half = jnp.stack(near[:2]), jnp.stack(near[2:])
    keep = jnp.where(place.high, high_half, low_half)
    send = jnp.where(place.high, low_half, high_half)
    groups = [keep, swap(send, "sub"), swap(keep, "expert"), far_both(send)]
    return groups, [[0, 0], [1, 1], [2, 2], [3, 3]], [keep, send]


def gather_rows(place, rows):
    count = rows.shape[0]
    whole = lax.all_gather(rows, ("tensor", "expert"))
    whole = whole.reshape(place.tensors, place.sources, count, rows.shape[1])
    whole = whole.transpose(1, 2, 0, 3).reshape(place.sources, count, 2, -1)
    halves = (whole[:, :, 0], whole[:, :, 1])
    first = place.sub == 0
    keep = jnp.where(first, halves[0], halves[1])
    got = swap(jnp.where(first, halves[1], halves[0]), "sub")
    both = jnp.where(first, jnp.stack([keep, got], 1), jnp.stack([got, keep], 1))
    both = both.reshape((2 * place.sources, count, -1))
    return [both], [list(range(2 * place.sources))]


def send_x(place, parts):
    kept, core_near, same_far, core_far = parts
    return kept, swap(core_near, "sub"), swap(same_far, "expert"), far_both(core_far)


def sum_x(place, terms):
    kept, from_core, from_far, from_both = (term.astype(F32) for term in terms)
    own_half, other_half = kept + from_far, from_core + from_both
    return [
        jnp.where(place.high, other_half, own_half).astype(BF16),
        jnp.where(place.high, own_half, other_half).astype(BF16),
    ]


def send_z(near, far, near_next, far_next):
    return near, across(far, 2), across(near_next, 1), across(far_next, 3)


def sum_z(terms):
    return functools.reduce(jnp.add, [term.astype(F32) for term in terms]).astype(BF16)


def scatter_rows(place, parts):
    stacked = jnp.stack(parts)
    count, half = stacked.shape[1:]
    stacked = stacked.reshape(place.sources, 2, count, half)
    first = place.sub == 0
    keep = jnp.where(first, stacked[:, 0], stacked[:, 1])
    got = swap(jnp.where(first, stacked[:, 1], stacked[:, 0]), "sub")
    both = jnp.where(first, jnp.concatenate([keep, got], 2), jnp.concatenate([got, keep], 2))
    both = both.reshape(place.sources, count, place.tensors, -1).transpose(0, 2, 1, 3)
    share = lax.psum_scatter(both, "expert", scatter_dimension=0)
    return lax.psum_scatter(share, "tensor", scatter_dimension=0)


def route_rows(small, locals_, index, meta_ref, take_ref, gate_ref):
    rows = meta_ref.shape[2]
    row, column = (lax.broadcasted_iota(jnp.int32, (rows, rows), axis) for axis in (0, 1))
    before = jnp.where(row < column, 1.0, 0.0).astype(BF16)
    slot = lax.broadcasted_iota(jnp.int32, (CAP, rows), 0).astype(F32)
    for place_at in range(meta_ref.shape[0]):
        start = block_at(small, index, place_at)[1]
        meta = meta_ref[place_at]
        for local in range(locals_):
            number = (index[0] * locals_ + local).astype(F32)
            one, two = meta[0:1] == number, meta[1:2] == number
            named = jnp.where(one | two, 1.0, 0.0)
            rank = jnp.dot(
                jnp.broadcast_to(named, (16, rows)).astype(BF16), before, preferred_element_type=F32
            )
            take = jnp.where(jnp.where(one | two, rank[0:1], -1.0) == slot, 1.0, 0.0)
            gate = jnp.where(one, meta[2:3], 0.0) + jnp.where(two, meta[3:4], 0.0)
            take_ref[local, place_at] = take.astype(BF16)
            gate_ref[local, pl.ds(start, CAP), :] = jnp.sum(take * gate, axis=1, keepdims=True)


def place_rows(small, index, take_ref, local, groups, places, rows_ref):
    width = groups[0].shape[2]
    seen = {}
    for group, held in zip(groups, places, strict=True):
        for i, place_at in enumerate(held):
            chunk = seen[place_at] = seen.get(place_at, -1) + 1
            start = block_at(small, index, place_at)[1]
            column = pl.multiple_of(other(lax.rem(index[2], 2), chunk) * width, 128) if small else 0
            rows_ref[pl.ds(start, CAP), pl.ds(column, width)] = jnp.dot(
                take_ref[local, place_at], group[i], preferred_element_type=F32
            ).astype(BF16)


def combine_rows(small, index, take_ref, slots_of, outs):
    half, width = slots_of[0].shape[1], outs[0].shape[1]
    chunks = 2 if small else 1
    places = len(outs) * width // half
    for place_at in range(places):
        start = block_at(small, index, place_at)[1]
        for chunk in range(chunks):
            span = half // chunks
            column = pl.multiple_of(other(lax.rem(index[2], 2), chunk) * span, 128) if small else 0
            total = None
            for local, slots in enumerate(slots_of):
                term = lax.dot_general(
                    take_ref[local, place_at], slots[pl.ds(start, CAP), pl.ds(column, span)],
                    (((0,), (0,)), ((), ())), preferred_element_type=F32,
                )
                total = term if total is None else total + term
            if width == half:
                outs[place_at][:, chunk * span : (chunk + 1) * span] = total.astype(BF16)
            else:
                outs[chunk * places + place_at][...] = total.astype(BF16)


class Stream:
    def __init__(self, arrays, places, tile, rings, sems):
        self.arrays, self.places, self.tile, self.rings, self.sems = arrays, places, tile, rings, sems
        self.depth = rings[0].shape[0]

    def copies(self, step):
        slot = lax.rem(step, self.depth)
        cut = pl.ds(pl.multiple_of(step * self.tile, self.tile), self.tile)
        return [
            pltpu.make_async_copy(array.at[place(cut)], ring.at[slot], self.sems.at[i, slot])
            for i, (array, place, ring) in enumerate(zip(self.arrays, self.places, self.rings, strict=True))
        ]

    def start(self, steps):
        for step in range(min(self.depth - 1, steps)):
            for copy in self.copies(step):
                copy.start()

    def take(self, step):
        @pl.when(step + self.depth - 1 < pl.num_programs(0))
        def _():
            for copy in self.copies(step + self.depth - 1):
                copy.start()

        for copy in self.copies(step):
            copy.wait()
        return [ring.at[lax.rem(step, self.depth)] for ring in self.rings]


def column_tile(local):
    return lambda cut: (local, slice(None), cut)


def pair_tile(cut):
    return slice(None), slice(None), cut


def one_tile(cut):
    return slice(None), cut


def first_body(small, local, locals_, places, n_routes, n_after, tile, steps, *refs):
    routes, refs = refs[:n_routes], refs[n_routes + n_after :]
    groups, (gate_w, up_w, out, *routed, rows, gate_ring, up_ring, sems) = refs[: len(places)], refs[len(places) :]
    take_ref = routes[0] if local else routed[0]
    stream = Stream([gate_w, up_w], [column_tile(local)] * 2, tile, [gate_ring, up_ring], sems)
    step = pl.program_id(0)

    @pl.when(step == 0)
    def _():
        stream.start(steps)
        if not local:
            route_rows(small, locals_, axis_indices(), *routes, *routed)
        place_rows(small, axis_indices(), take_ref, local, groups, places, rows)

    for i, weight in enumerate(stream.take(step)):
        out[i] = jnp.dot(rows[...], weight[...], preferred_element_type=F32).astype(BF16)


def middle_body(small, local, locals_, places, tile, steps, take_ref, gate_ref, *refs):
    groups, refs = refs[: len(places)], refs[len(places) :]
    last = local == locals_ - 1
    before, refs = (refs[:local], refs[local:]) if last else ((), refs)
    own_at, got_at, down, slopes, back, *outs, rows, total, slots, own_ring, got_ring, ring, sems = refs
    stream = Stream(
        [down, own_at, got_at], [lambda cut: (local, cut), pair_tile, pair_tile], tile, [ring, own_ring, got_ring], sems
    )
    step = pl.program_id(0)

    @pl.when(step == 0)
    def _():
        stream.start(steps)
        place_rows(small, axis_indices(), take_ref, local, groups, places, rows)
        total[...] = jnp.zeros_like(total)

    weight, own, got = stream.take(step)
    back[...] = nt(rows[...], weight[...]).astype(BF16)
    gate_pre = own[0].astype(F32) + got[0].astype(F32)
    up_pre = own[1].astype(F32) + got[1].astype(F32)
    sigmoid = 0.5 * jnp.tanh(0.5 * gate_pre) + 0.5
    silu = gate_pre * sigmoid
    hidden = (silu * up_pre).astype(BF16)
    slopes[0] = silu.astype(BF16)
    slopes[1] = (up_pre * (sigmoid + silu * (1.0 - sigmoid))).astype(BF16)
    total[...] += jnp.dot(hidden, weight[...], preferred_element_type=F32)

    @pl.when(step == pl.num_programs(0) - 1)
    def _():
        finish(small, last, take_ref, gate_ref[local], before, total, slots, outs)


def last_body(small, local, locals_, n_after, tile, steps, take_ref, gate_ref, *refs):
    refs = refs[n_after:]
    last = local == locals_ - 1
    before, refs = (refs[:local], refs[local:]) if last else ((), refs)
    own_at, got_at, slopes_at, gate_w, up_w, *outs, total, slots, own_ring, got_ring, slope_ring, gate_ring, up_ring, sems = refs
    stream = Stream(
        [own_at, got_at, slopes_at, gate_w, up_w], [one_tile, one_tile, pair_tile, *[column_tile(local)] * 2], tile,
        [own_ring, got_ring, slope_ring, gate_ring, up_ring], sems,
    )
    step = pl.program_id(0)

    @pl.when(step == 0)
    def _():
        stream.start(steps)
        total[...] = jnp.zeros_like(total)

    own, got, slopes, gate_tile, up_tile = stream.take(step)
    back = own[...].astype(F32) + got[...].astype(F32)
    up_grad = (back * slopes[0].astype(F32)).astype(BF16)
    gate_grad = (back * slopes[1].astype(F32)).astype(BF16)
    total[...] += nt(gate_grad, gate_tile[...]) + nt(up_grad, up_tile[...])

    @pl.when(step == pl.num_programs(0) - 1)
    def _():
        finish(small, last, take_ref, gate_ref[local], before, total, slots, outs)


def finish(small, last, take_ref, gate, before, total, slots, outs):
    weighted = (total[...] * gate).astype(BF16)
    if last:
        slots[...] = weighted
        combine_rows(small, axis_indices(), take_ref, [*before, slots], outs)
    else:
        outs[0][...] = weighted


def whole(array):
    dims = len(array.shape)
    return pl.BlockSpec(array.shape, lambda f: (0,) * dims)


def call(body, steps, routes, after, near, near_specs, weights, outs, out_specs, scratch, flops):
    anywhere = pl.BlockSpec(memory_space=pl.ANY)
    return pl.pallas_call(
        body,
        grid=(steps,),
        in_specs=[*map(whole, routes), *[anywhere] * len(after), *near_specs,
                  *[anywhere] * len(weights)],
        out_specs=out_specs,
        out_shape=outs,
        scratch_shapes=scratch,
        compiler_params=pltpu.CompilerParams(vmem_limit_bytes=VMEM_BYTES),
        cost_estimate=pl.CostEstimate(flops=flops, bytes_accessed=1000, transcendentals=0),
    )(*routes, *after, *near, *weights)


def in_hbm(*arrays):
    return [pltpu.with_memory_space_constraint(array, pltpu.HBM) for array in arrays]


def per_device(tokens, cotangent, expert_ids, gate_values, w_gate, w_up, w_down):
    place = Place()
    small, blocks = place.small, place.blocks
    locals_, half, hidden = w_gate.shape
    count = tokens.shape[0]
    slots = blocks * CAP
    flops = 2 * slots * half * hidden

    meta = jnp.concatenate([expert_ids.astype(F32).T, gate_values.T, jnp.zeros((4, count), F32)])
    meta = gather_meta(place, meta)
    routed = [jax.ShapeDtypeStruct((locals_, blocks, CAP, count), BF16),
              jax.ShapeDtypeStruct((locals_, slots, 1), F32)]

    if small:
        token_groups, token_places, token_last, meta = gather_now(place, tokens, meta)
        grad_near = gather_first(cotangent, token_last)
    else:
        token_groups, token_places = gather_rows(place, tokens)
        grad_groups, grad_places = gather_rows(place, cotangent)

    tile = min(TILE, hidden)
    steps = hidden // tile
    pair = pltpu.HBM((2, slots, hidden), BF16)
    one = pltpu.HBM((slots, hidden), BF16)
    pair_spec = pl.BlockSpec((2, slots, tile), lambda f: (0, 0, f))
    one_spec = pl.BlockSpec((slots, tile), lambda f: (0, f))
    pair_ring, one_ring = pltpu.VMEM((DEPTH, 2, slots, tile), BF16), pltpu.VMEM((DEPTH, slots, tile), BF16)

    def sems(arrays):
        return pltpu.SemaphoreType.DMA((arrays, DEPTH))


    def ends(local, width):
        return [jax.ShapeDtypeStruct((count, width), BF16)] * (blocks * half // width) if local == locals_ - 1 else [
            jax.ShapeDtypeStruct((slots, width), BF16)]

    own_pre, got_pre, after = [], [], []
    for local in range(locals_):
        ring = pltpu.VMEM((DEPTH, half, tile), BF16)
        routes, new = ([take], []) if local else ([meta], routed)
        own, *new = call(
            functools.partial(first_body, small, local, locals_, token_places, len(routes), len(after), tile, steps),
            steps, routes, after, token_groups, [*map(whole, token_groups)], [w_gate, w_up],
            [pair, *new], [pair_spec, *map(whole, new)], [pltpu.VMEM((slots, half), BF16), ring, ring, sems(2)],
            COST * flops if local else FIRST_COST,
        )
        if not local:
            take, gate = new
        own_pre.append(own)
        got_pre.append(swap(own, "sub"))
        if small and local == 0:
            grad_groups, grad_places, after = gather_last(place, grad_near, own)

    done, own_back, got_back, slopes = [], [], [], []
    for local in range(locals_):
        before = done if local == locals_ - 1 else []
        outs = ends(local, half)
        slope, back, *mixed_parts = call(
            functools.partial(middle_body, small, local, locals_, grad_places, tile, steps),
            steps, [take, gate], [], [*grad_groups, *before], [*map(whole, [*grad_groups, *before])],
            [*in_hbm(own_pre[local], got_pre[local]), w_down],
            [pair, one, *outs], [pair_spec, one_spec, *map(whole, outs)],
            [pltpu.VMEM((slots, half), BF16), pltpu.VMEM((slots, half), F32), pltpu.VMEM((slots, half), BF16),
             pair_ring, pair_ring, pltpu.VMEM((DEPTH, tile, half), BF16), sems(3)],
            COST * flops,
        )
        slopes.append(slope)
        own_back.append(back)
        got_back.append(swap(back, "sub"))
        done.append(mixed_parts[0])

    ring = pltpu.VMEM((DEPTH, half, tile), BF16)
    done, after = [], []
    mixed_terms = send_x(place, mixed_parts) if small else []
    for local in range(locals_):
        last = local == locals_ - 1
        before = done if last else []
        outs = ends(local, half // 2 if small and last else half)
        grad_parts = call(
            functools.partial(last_body, small, local, locals_, len(after), tile, steps),
            steps, [take, gate], after, before, [*map(whole, before)],
            [*in_hbm(own_back[local], got_back[local], slopes[local]), w_gate, w_up],
            outs, [*map(whole, outs)],
            [pltpu.VMEM((slots, half), F32), pltpu.VMEM((slots, half), BF16), one_ring, one_ring, pair_ring, ring, ring,
             sems(5)],
            COST * flops,
        )
        done.append(grad_parts[0])
    if not small:
        return scatter_rows(place, mixed_parts), scatter_rows(place, grad_parts)
    next_terms = send_x(place, grad_parts[blocks:])
    last_terms = send_x(place, grad_parts[:blocks])

    *mixed_terms, _ = lax.optimization_barrier((*mixed_terms, grad_parts[0]))
    mixed_terms = [[term[:, i * half // 2 : (i + 1) * half // 2] for term in mixed_terms] for i in range(2)]
    (near, far), (near_next, far_next) = (sum_x(place, terms) for terms in mixed_terms)
    got = across(jnp.stack([near_next, far]), 1)
    rest = (far_next.astype(F32) + got[1].astype(F32)).astype(BF16)
    *next_terms, rest = lax.optimization_barrier((*next_terms, rest))
    mixed = sum_z((near, got[0], across(rest, 3)))
    return mixed, sum_z(send_z(*sum_x(place, last_terms), *sum_x(place, next_terms)))


def solution(mesh):
    rows = P(("groups", "expert", "sub"), "tensor")
    ids = P(("groups", "expert", "sub"), None)
    return jax.shard_map(
        per_device,
        mesh=mesh,
        in_specs=(rows, rows, ids, ids, P("expert", "sub", "tensor"), P("expert", "sub", "tensor"),
                  P("expert", "tensor", "sub")),
        out_specs=(rows, rows),
        check_vma=False,
    )
```

```python
import functools

import jax
import jax.numpy as jnp
from jax import lax
from jax.experimental import pallas as pl
from jax.experimental.pallas import tpu as pltpu
from jax.sharding import PartitionSpec as P

EXPERTS = 4
CAP = 80
BF16 = jnp.bfloat16
F32 = jnp.float32
VMEM_BYTES = 36 * 1024 * 1024
TILE = 512
DEPTH = 3
COST = 50
FIRST_COST = 1000


def swap(value, axis):
    return lax.ppermute(value, axis, [(0, 1), (1, 0)])


def across(value, distance):
    return lax.ppermute(value, "tensor", [(i, i ^ distance) for i in range(lax.axis_size("tensor"))])


def nt(a, b):
    return lax.dot_general(a, b, (((1,), (1,)), ((), ())), preferred_element_type=F32)


class Place:
    def __init__(self):
        self.sources = lax.axis_size("expert")
        self.tensors = lax.axis_size("tensor")
        self.small = self.sources == 2 and self.tensors == 4
        self.expert = lax.axis_index("expert")
        self.sub = lax.axis_index("sub")
        self.tensor = lax.axis_index("tensor")
        self.high = (self.tensor // 2 + self.sub) % 2 == 1
        self.blocks = 2 * self.sources


def other(index, far):
    return index + far - 2 * index * far


def axis_indices():
    return tuple(lax.axis_index(axis) for axis in ("expert", "sub", "tensor"))


def block_at(small, index, place_at):
    if not small:
        return place_at, place_at * CAP
    block = other(index[0], place_at // 2) * 2 + other(index[1], place_at % 2)
    return block, pl.multiple_of(block * CAP, 16)


def far_both(value):
    return lax.ppermute(value, ("expert", "sub"), [(i, 3 - i) for i in range(4)])


def gather_meta(place, meta):
    if place.small:
        pair = jnp.stack([meta, swap(meta, "sub")])
        return jnp.concatenate([pair, swap(pair, "expert")])
    return lax.all_gather(meta, ("expert", "sub"))


def gather_now(place, rows, meta):
    near = [rows] + [across(rows, k) for k in (1, 2, 3)]
    near[3], meta = lax.optimization_barrier((near[3], meta))
    far = [swap(block, "expert") for block in near]
    low_half = jnp.stack([near[0], near[1], far[0], far[1]])
    high_half = jnp.stack([near[2], near[3], far[2], far[3]])
    keep = jnp.where(place.high, high_half, low_half)
    send = jnp.where(place.high, low_half, high_half)
    return [keep, swap(send, "sub")], [[0, 0, 2, 2], [1, 1, 3, 3]], near[3], meta


def gather_first(rows, after):
    rows, _ = lax.optimization_barrier((rows, after))
    return [rows] + [across(rows, k) for k in (1, 2, 3)]


def gather_last(place, near, after):
    *near, _ = lax.optimization_barrier((*near, after))
    low_half, high_half = jnp.stack(near[:2]), jnp.stack(near[2:])
    keep = jnp.where(place.high, high_half, low_half)
    send = jnp.where(place.high, low_half, high_half)
    groups = [keep, swap(send, "sub"), swap(keep, "expert"), far_both(send)]
    return groups, [[0, 0], [1, 1], [2, 2], [3, 3]], [keep, send]


def gather_rows(place, rows):
    count = rows.shape[0]
    whole = lax.all_gather(rows, ("tensor", "expert"))
    whole = whole.reshape(place.tensors, place.sources, count, rows.shape[1])
    whole = whole.transpose(1, 2, 0, 3).reshape(place.sources, count, 2, -1)
    halves = (whole[:, :, 0], whole[:, :, 1])
    first = place.sub == 0
    keep = jnp.where(first, halves[0], halves[1])
    got = swap(jnp.where(first, halves[1], halves[0]), "sub")
    both = jnp.where(first, jnp.stack([keep, got], 1), jnp.stack([got, keep], 1))
    both = both.reshape((2 * place.sources, count, -1))
    return [both], [list(range(2 * place.sources))]


def send_x(place, parts):
    kept, core_near, same_far, core_far = parts
    return kept, swap(core_near, "sub"), swap(same_far, "expert"), far_both(core_far)


def sum_x(place, terms):
    kept, from_core, from_far, from_both = (term.astype(F32) for term in terms)
    own_half, other_half = kept + from_far, from_core + from_both
    return [
        jnp.where(place.high, other_half, own_half).astype(BF16),
        jnp.where(place.high, own_half, other_half).astype(BF16),
    ]


def send_z(near, far, near_next, far_next):
    return near, across(far, 2), across(near_next, 1), across(far_next, 3)


def sum_z(terms):
    return functools.reduce(jnp.add, [term.astype(F32) for term in terms]).astype(BF16)


def scatter_rows(place, parts):
    stacked = jnp.stack(parts)
    count, half = stacked.shape[1:]
    stacked = stacked.reshape(place.sources, 2, count, half)
    first = place.sub == 0
    keep = jnp.where(first, stacked[:, 0], stacked[:, 1])
    got = swap(jnp.where(first, stacked[:, 1], stacked[:, 0]), "sub")
    both = jnp.where(first, jnp.concatenate([keep, got], 2), jnp.concatenate([got, keep], 2))
    both = both.reshape(place.sources, count, place.tensors, -1).transpose(0, 2, 1, 3)
    share = lax.psum_scatter(both, "expert", scatter_dimension=0)
    return lax.psum_scatter(share, "tensor", scatter_dimension=0)


def route_rows(small, locals_, index, meta_ref, take_ref, gate_ref):
    rows = meta_ref.shape[2]
    row, column = (lax.broadcasted_iota(jnp.int32, (rows, rows), axis) for axis in (0, 1))
    before = jnp.where(row < column, 1.0, 0.0).astype(BF16)
    slot = lax.broadcasted_iota(jnp.int32, (CAP, rows), 0).astype(F32)
    for place_at in range(meta_ref.shape[0]):
        start = block_at(small, index, place_at)[1]
        meta = meta_ref[place_at]
        for local in range(locals_):
            number = (index[0] * locals_ + local).astype(F32)
            one, two = meta[0:1] == number, meta[1:2] == number
            named = jnp.where(one | two, 1.0, 0.0)
            rank = jnp.dot(
                jnp.broadcast_to(named, (16, rows)).astype(BF16), before, preferred_element_type=F32
            )
            take = jnp.where(jnp.where(one | two, rank[0:1], -1.0) == slot, 1.0, 0.0)
            gate = jnp.where(one, meta[2:3], 0.0) + jnp.where(two, meta[3:4], 0.0)
            take_ref[local, place_at] = take.astype(BF16)
            weight = jnp.sum(take * gate, axis=1, keepdims=True)
            gate_ref[local, pl.ds(start, CAP), :] = jnp.broadcast_to(weight, (CAP, 128))


def place_rows(small, index, take_ref, local, groups, places, rows_ref):
    width = groups[0].shape[2]
    seen = {}
    for group, held in zip(groups, places, strict=True):
        for i, place_at in enumerate(held):
            chunk = seen[place_at] = seen.get(place_at, -1) + 1
            start = block_at(small, index, place_at)[1]
            column = pl.multiple_of(other(lax.rem(index[2], 2), chunk) * width, 128) if small else 0
            rows_ref[pl.ds(start, CAP), pl.ds(column, width)] = jnp.dot(
                take_ref[local, place_at], group[i], preferred_element_type=F32
            ).astype(BF16)


def combine_rows(small, index, take_ref, slots_of, outs):
    half, width = slots_of[0].shape[1], outs[0].shape[1]
    chunks = 2 if small else 1
    places = len(outs) * width // half
    for place_at in range(places):
        start = block_at(small, index, place_at)[1]
        takes = jnp.concatenate([take_ref[local, place_at] for local in range(len(slots_of))])
        for chunk in range(chunks):
            span = half // chunks
            column = pl.multiple_of(other(lax.rem(index[2], 2), chunk) * span, 128) if small else 0
            total = lax.dot_general(
                takes, jnp.concatenate([slots[pl.ds(start, CAP), pl.ds(column, span)] for slots in slots_of]),
                (((0,), (0,)), ((), ())), preferred_element_type=F32,
            )
            if width == half:
                outs[place_at][:, chunk * span : (chunk + 1) * span] = total.astype(BF16)
            else:
                outs[chunk * places + place_at][...] = total.astype(BF16)


class Stream:
    def __init__(self, arrays, places, tile, rings, sems):
        self.arrays, self.places, self.tile, self.rings, self.sems = arrays, places, tile, rings, sems
        self.depth = rings[0].shape[0]

    def copies(self, step):
        slot = lax.rem(step, self.depth)
        cut = pl.ds(pl.multiple_of(step * self.tile, self.tile), self.tile)
        return [
            pltpu.make_async_copy(array.at[place(cut)], ring.at[slot], self.sems.at[i, slot])
            for i, (array, place, ring) in enumerate(zip(self.arrays, self.places, self.rings, strict=True))
        ]

    def start(self, steps):
        for step in range(min(self.depth - 1, steps)):
            for copy in self.copies(step):
                copy.start()

    def take(self, step):
        @pl.when(step + self.depth - 1 < pl.num_programs(0))
        def _():
            for copy in self.copies(step + self.depth - 1):
                copy.start()

        for copy in self.copies(step):
            copy.wait()
        return [ring.at[lax.rem(step, self.depth)] for ring in self.rings]


def column_tile(local):
    return lambda cut: (local, slice(None), cut)


def pair_tile(cut):
    return slice(None), slice(None), cut


def one_tile(cut):
    return slice(None), cut


def first_body(small, local, locals_, places, tile, steps, start_late, wait_early, wait_late, route, *refs):
    groups, (gate_w, up_w, out, *routed, rows, gate_ring, up_ring, sems) = refs[: len(places)], refs[len(places) :]
    take_ref = route if local else routed[0]
    stream = Stream([gate_w, up_w], [column_tile(local)] * 2, tile, [gate_ring, up_ring], sems)
    step = pl.program_id(0)

    @pl.when(step == 0)
    def _():
        stream.start(steps)
        start_late()
        wait_early()
        if not local:
            route_rows(small, locals_, axis_indices(), route, *routed)
        place_rows(small, axis_indices(), take_ref, local, groups, places, rows)

    for i, weight in enumerate(stream.take(step)):
        out[i] = jnp.dot(rows[...], weight[...], preferred_element_type=F32).astype(BF16)


def middle_body(small, local, locals_, places, tile, steps, start_late, wait_early, wait_late, take_ref, *refs):
    groups, gate_ref, refs = refs[: len(places)], refs[len(places)], refs[len(places) + 1 :]
    last = local == locals_ - 1
    before, refs = (refs[:local], refs[local:]) if last else ((), refs)
    own_at, got_at, down, slopes, back, *outs, rows, total, slots, own_ring, got_ring, ring, sems = refs
    stream = Stream(
        [down, own_at, got_at], [lambda cut: (local, cut), pair_tile, pair_tile], tile, [ring, own_ring, got_ring], sems
    )
    step = pl.program_id(0)

    @pl.when(step == 0)
    def _():
        start_late()
        stream.start(steps)
        wait_early()
        place_rows(small, axis_indices(), take_ref, local, groups, places, rows)
        total[...] = jnp.zeros_like(total)

    weight, own, got = stream.take(step)
    back[...] = nt(rows[...], weight[...]).astype(BF16)
    gate_pre = own[0].astype(F32) + got[0].astype(F32)
    up_pre = own[1].astype(F32) + got[1].astype(F32)
    sigmoid = 0.5 * jnp.tanh(0.5 * gate_pre) + 0.5
    silu = gate_pre * sigmoid
    hidden = (silu * up_pre).astype(BF16)
    slopes[0] = silu.astype(BF16)
    slopes[1] = (up_pre * (sigmoid + silu * (1.0 - sigmoid))).astype(BF16)
    total[...] += jnp.dot(hidden, weight[...], preferred_element_type=F32)

    @pl.when(step == pl.num_programs(0) - 1)
    def _():
        wait_late()
        finish(small, last, take_ref, gate_ref[local][:, :1], before, total, slots, outs)


def last_body(small, local, locals_, tile, steps, start_late, wait_early, wait_late, gate_ref, *refs):
    last = local == locals_ - 1
    (take_ref, *before), refs = (refs[: local + 1], refs[local + 1 :]) if last else ((None,), refs)
    own_at, got_at, slopes_at, gate_w, up_w, *outs, total, slots, own_ring, got_ring, slope_ring, gate_ring, up_ring, sems = refs
    stream = Stream(
        [own_at, got_at, slopes_at, gate_w, up_w], [one_tile, one_tile, pair_tile, *[column_tile(local)] * 2], tile,
        [own_ring, got_ring, slope_ring, gate_ring, up_ring], sems,
    )
    step = pl.program_id(0)

    @pl.when(step == 0)
    def _():
        stream.start(steps)
        start_late()
        total[...] = jnp.zeros_like(total)

    own, got, slopes, gate_tile, up_tile = stream.take(step)
    back = own[...].astype(F32) + got[...].astype(F32)
    up_grad = (back * slopes[0].astype(F32)).astype(BF16)
    gate_grad = (back * slopes[1].astype(F32)).astype(BF16)
    total[...] += nt(gate_grad, gate_tile[...]) + nt(up_grad, up_tile[...])

    @pl.when(step == pl.num_programs(0) - 1)
    def _():
        wait_late()
        finish(small, last, take_ref, gate_ref[local][:, :1], before, total, slots, outs)


def finish(small, last, take_ref, gate, before, total, slots, outs):
    weighted = (total[...] * gate).astype(BF16)
    if last:
        slots[...] = weighted
        combine_rows(small, axis_indices(), take_ref, [*before, slots], outs)
    else:
        outs[0][...] = weighted


def whole(array):
    dims = len(array.shape)
    return pl.BlockSpec(array.shape, lambda f: (0,) * dims)


def call(body, steps, early, after, late, weights, outs, out_specs, scratch, flops):
    near = [*early, *late]

    def run(*refs):
        sources, refs, held, near_sems = refs[: len(near)], refs[len(near) + len(after) : -len(near) - 1], refs[
            -len(near) - 1 : -1], refs[-1]
        copies = [pltpu.make_async_copy(sources[i], held[i], near_sems.at[i]) for i in range(len(near))]

        @pl.when(pl.program_id(0) == 0)
        def _():
            for copy in copies[: len(early)]:
                copy.start()

        def start_late():
            for copy in copies[len(early) :]:
                copy.start()

        def wait_early():
            for copy in copies[: len(early)]:
                copy.wait()

        def wait_late():
            for copy in copies[len(early) :]:
                copy.wait()

        body(start_late, wait_early, wait_late, *held, *refs)

    return pl.pallas_call(
        run,
        grid=(steps,),
        in_specs=[pl.BlockSpec(memory_space=pl.ANY)] * (len(near) + len(after) + len(weights)),
        out_specs=out_specs,
        out_shape=outs,
        scratch_shapes=[*scratch, *[pltpu.VMEM(array.shape, array.dtype) for array in near],
                        pltpu.SemaphoreType.DMA((len(near),))],
        compiler_params=pltpu.CompilerParams(vmem_limit_bytes=VMEM_BYTES),
        cost_estimate=pl.CostEstimate(flops=flops, bytes_accessed=1000, transcendentals=0),
    )(*near, *after, *weights)


def in_hbm(*arrays):
    return [pltpu.with_memory_space_constraint(array, pltpu.HBM) for array in arrays]


def per_device(tokens, cotangent, expert_ids, gate_values, w_gate, w_up, w_down):
    place = Place()
    small, blocks = place.small, place.blocks
    locals_, half, hidden = w_gate.shape
    count = tokens.shape[0]
    slots = blocks * CAP
    flops = 2 * slots * half * hidden

    meta = jnp.concatenate([expert_ids.astype(F32).T, gate_values.T, jnp.zeros((4, count), F32)])
    meta = gather_meta(place, meta)
    routed = [jax.ShapeDtypeStruct((locals_, blocks, CAP, count), BF16),
              jax.ShapeDtypeStruct((locals_, slots, 128), F32)]

    if small:
        token_groups, token_places, token_last, meta = gather_now(place, tokens, meta)
        grad_near = gather_first(cotangent, token_last)
    else:
        token_groups, token_places = gather_rows(place, tokens)
        grad_groups, grad_places = gather_rows(place, cotangent)

    tile = min(TILE, hidden)
    steps = hidden // tile
    pair = pltpu.HBM((2, slots, hidden), BF16)
    one = pltpu.HBM((slots, hidden), BF16)
    pair_spec = pl.BlockSpec((2, slots, tile), lambda f: (0, 0, f))
    one_spec = pl.BlockSpec((slots, tile), lambda f: (0, f))
    pair_ring, one_ring = pltpu.VMEM((DEPTH, 2, slots, tile), BF16), pltpu.VMEM((DEPTH, slots, tile), BF16)

    def sems(arrays):
        return pltpu.SemaphoreType.DMA((arrays, DEPTH))


    def ends(local, width):
        return [jax.ShapeDtypeStruct((count, width), BF16)] * (blocks * half // width) if local == locals_ - 1 else [
            jax.ShapeDtypeStruct((slots, width), BF16)]

    own_pre, got_pre, after = [], [], []
    for local in range(locals_):
        ring = pltpu.VMEM((DEPTH, half, tile), BF16)
        route, new = (take, []) if local else (meta, routed)
        own, *new = call(
            functools.partial(first_body, small, local, locals_, token_places, tile, steps),
            steps, [route, *token_groups], after, [], [w_gate, w_up],
            [pair, *new], [pair_spec, *map(whole, new)], [pltpu.VMEM((slots, half), BF16), ring, ring, sems(2)],
            COST * flops if local else FIRST_COST,
        )
        if not local:
            take, gate = new
        own_pre.append(own)
        got_pre.append(swap(own, "sub"))
        if small and local == 0:
            grad_groups, grad_places, after = gather_last(place, grad_near, own)

    done, own_back, got_back, slopes = [], [], [], []
    for local in range(locals_):
        before = done if local == locals_ - 1 else []
        outs = ends(local, half)
        slope, back, *mixed_parts = call(
            functools.partial(middle_body, small, local, locals_, grad_places, tile, steps),
            steps, [take, *grad_groups], [], [gate, *before],
            [*in_hbm(own_pre[local], got_pre[local]), w_down],
            [pair, one, *outs], [pair_spec, one_spec, *map(whole, outs)],
            [pltpu.VMEM((slots, half), BF16), pltpu.VMEM((slots, half), F32), pltpu.VMEM((slots, half), BF16),
             pair_ring, pair_ring, pltpu.VMEM((DEPTH, tile, half), BF16), sems(3)],
            COST * flops,
        )
        slopes.append(slope)
        own_back.append(back)
        got_back.append(swap(back, "sub"))
        done.append(mixed_parts[0])

    ring = pltpu.VMEM((DEPTH, half, tile), BF16)
    done = []
    mixed_terms = send_x(place, mixed_parts) if small else []
    for local in range(locals_):
        last = local == locals_ - 1
        before = done if last else []
        outs = ends(local, half // 2 if small and last else half)
        grad_parts = call(
            functools.partial(last_body, small, local, locals_, tile, steps),
            steps, [], [], [gate, take, *before] if last else [gate],
            [*in_hbm(own_back[local], got_back[local], slopes[local]), w_gate, w_up],
            outs, [*map(whole, outs)],
            [pltpu.VMEM((slots, half), F32), pltpu.VMEM((slots, half), BF16), one_ring, one_ring, pair_ring, ring, ring,
             sems(5)],
            COST * flops,
        )
        done.append(grad_parts[0])
    if not small:
        return scatter_rows(place, mixed_parts), scatter_rows(place, grad_parts)
    next_terms = send_x(place, grad_parts[blocks:])
    last_terms = send_x(place, grad_parts[:blocks])

    *mixed_terms, _ = lax.optimization_barrier((*mixed_terms, grad_parts[0]))
    mixed_terms = [[term[:, i * half // 2 : (i + 1) * half // 2] for term in mixed_terms] for i in range(2)]
    (near, far), (near_next, far_next) = (sum_x(place, terms) for terms in mixed_terms)
    got = across(jnp.stack([near_next, far]), 1)
    rest = (far_next.astype(F32) + got[1].astype(F32)).astype(BF16)
    *next_terms, rest = lax.optimization_barrier((*next_terms, rest))
    mixed = sum_z((near, got[0], across(rest, 3)))
    return mixed, sum_z(send_z(*sum_x(place, last_terms), *sum_x(place, next_terms)))


def solution(mesh):
    rows = P(("groups", "expert", "sub"), "tensor")
    ids = P(("groups", "expert", "sub"), None)
    return jax.shard_map(
        per_device,
        mesh=mesh,
        in_specs=(rows, rows, ids, ids, P("expert", "sub", "tensor"), P("expert", "sub", "tensor"),
                  P("expert", "tensor", "sub")),
        out_specs=(rows, rows),
        check_vma=False,
    )
```
